32 devices in a mesh: rec: 2 (over y), tm: 4 (over z), state: 2 (over x), sens: 2 (over core).
Axes of the slice: x: 2, y: 2, z: 4, core: 2. Of those that a mesh axis runs over, the one named last changes fastest.
Arguments:
- observations: bfloat16 [512, 64, 1024], P(('rec', 'state'), 'tm', 'sens'), parts along dimension 0, may hold values from -6 to 6
- obs_gain: bfloat16 [256, 1024], P(None, 'sens'), may hold values from -0.1875 to 0.1875
- closed_loop: float32 [256, 256], replicated, may hold values from -1 to 1
- transition: bfloat16 [256, 256], replicated, may hold values from -0.375 to 0.375
- smoother_gain: float32 [256, 256], replicated, may hold values from -1 to 1
- initial_mean: float32 [512, 256], P(('rec', 'state', 'sens')), parts along dimension 0, may hold values from -6 to 6
Outputs:
- filtered: float32 [512, 64, 256], P(('rec', 'state', 'sens'), 'tm'), parts along dimension 0
- smoothed: float32 [512, 64, 256], P(('rec', 'state', 'sens'), 'tm'), parts along dimension 0
The draws below stay inside these ranges and needn't reach their ends.
There are 2 independent parts, one for each index of `rec`. The reference program is written for one: setup_inputs(seed, part) draws one part's arguments, and reference() takes and returns one part's arrays. A program takes and returns all parts, laid end to end along the dimension named above; an argument that names none is the same for every part. Nothing has to cross between parts.
All inputs are finite; a program needn't handle non-finite values.
Results may differ from the reference program's by a relative error of at most 0.0036.
Values may be sent and summed in bfloat16 or wider, within the bound.
No kernel may reach another device: no remote copies, remote signals or barrier semaphores. Data moves between devices by JAX's collectives and lax.ppermute only.
A program may use at most 64 MiB of HBM per device.

```python
import math
import jax
import jax.numpy as jnp
from jax import lax

STATES = 256
SENSORS = 1024
BATCH = 256
STEPS = 64


def scaled_rotation(key, rate_low, rate_high):
    key_order, key_rows, key_cols, key_rates = jax.random.split(key, 4)
    row_index = jnp.arange(STATES, dtype=jnp.float32)[:, None]
    col_index = jnp.arange(STATES, dtype=jnp.float32)[None, :]
    cosine_rows = math.sqrt(2.0 / STATES) * jnp.cos(math.pi * (col_index + 0.5) * row_index / STATES)
    cosine_rows = cosine_rows * jnp.where(row_index == 0.0, math.sqrt(0.5), 1.0)
    shuffle = jax.random.permutation(key_order, STATES)
    cosine_rows = cosine_rows[shuffle]
    row_signs = jnp.where(jax.random.bernoulli(key_rows, 0.5, (STATES,)), 1.0, -1.0)
    col_signs = jnp.where(jax.random.bernoulli(key_cols, 0.5, (STATES,)), 1.0, -1.0)
    rates_log = jax.random.uniform(key_rates, (STATES,), jnp.float32, math.log(rate_low), math.log(rate_high))
    retained = 1.0 - jnp.exp(rates_log)
    return (retained * row_signs)[:, None] * cosine_rows * col_signs[None, :]


def draw_closed_loop(key, part):
    return scaled_rotation(jax.random.fold_in(key, 11), 0.0005, 0.02)


def draw_smoother_gain(key, part):
    return scaled_rotation(jax.random.fold_in(key, 23), 0.0005, 0.02)


def levels(own_key, shape, cuts, least, high):
    level = 1.0
    for dim, parts in cuts:
        heights = jax.random.uniform(jax.random.fold_in(jax.random.fold_in(own_key, 6), dim), (parts,), jnp.float32, least / len(cuts), high / len(cuts))
        level = level * jnp.repeat(jnp.exp(heights), shape[dim] // parts).reshape((-1,) + (1,) * (len(shape) - 1 - dim))
    return level


def noise(stream_key, dims, deviation, bound, cuts=(), held_as=jnp.bfloat16):
    array = jax.random.normal(stream_key, dims, jnp.float32) * deviation
    if len(cuts) > 0:
        array = levels(stream_key, dims, cuts, -0.22, 0.18) * array
    return jnp.clip(array, min=-bound, max=bound).astype(held_as)


def setup_inputs(seed: int = 0, part: int = 0) -> dict:
    arg_keys = jax.random.split(jax.random.key(seed), 7)
    own_keys = jax.random.split(jax.random.fold_in(arg_keys[6], part), 7)
    return {
        "observations": noise(own_keys[0], (BATCH, STEPS, SENSORS), 1.0, 6.0, ((0, 2), (1, 4), (2, 2))),
        "obs_gain": noise(arg_keys[1], (STATES, SENSORS), SENSORS ** -0.5, 0.1875, ((1, 2),)),
        "closed_loop": draw_closed_loop(jax.random.fold_in(arg_keys[6], 71), part),
        "transition": noise(arg_keys[3], (STATES, STATES), STATES ** -0.5, 0.375),
        "smoother_gain": draw_smoother_gain(jax.random.fold_in(arg_keys[6], 71), part),
        "initial_mean": noise(own_keys[5], (BATCH, STATES), 1.0, 6.0, ((0, 4),), jnp.float32),
    }


def reference(observations, obs_gain, closed_loop, transition, smoother_gain, initial_mean):
    highest = lax.Precision.HIGHEST
    inputs = jnp.einsum("bts,ks->tbk", observations.astype(jnp.float32), obs_gain.astype(jnp.float32), precision=highest)
    loop_t = closed_loop.T
    gain_t = smoother_gain.T

    def forward(state, term):
        fresh = jnp.dot(state, loop_t, precision=highest) + term
        return fresh, fresh

    _, filtered = lax.scan(forward, initial_mean, inputs)
    flat = filtered.reshape(-1, STATES)
    filtered_low = flat.astype(jnp.bfloat16)
    gain_low = smoother_gain.astype(jnp.bfloat16)
    predicted = jnp.dot(filtered_low, transition.T, preferred_element_type=jnp.float32).astype(jnp.bfloat16)
    adjusted = flat - jnp.dot(predicted, gain_low.T, preferred_element_type=jnp.float32)
    adjusted = adjusted.reshape(filtered.shape)

    def backward(state, term):
        fresh = term + jnp.dot(state, gain_t, precision=highest)
        return fresh, fresh

    _, earlier = lax.scan(backward, filtered[-1], adjusted[:-1], reverse=True)
    smoothed = jnp.concatenate([earlier, filtered[-1:]], 0)
    return jnp.swapaxes(filtered, 0, 1), jnp.swapaxes(smoothed, 0, 1)
```

```python
import jax
import jax.numpy as jnp
from jax import lax
from jax.experimental import pallas as pl
from jax.experimental.pallas import tpu as pltpu
from jax.sharding import PartitionSpec as P

F32 = jnp.float32
BF16 = jnp.bfloat16
LANES = 128
VMEM = pl.BlockSpec(memory_space=pltpu.VMEM)
SMEM = pl.BlockSpec(memory_space=pltpu.SMEM)
PARAMS = pltpu.CompilerParams(vmem_limit_bytes=40 * 2**20)


def halves(x):
    high = x.astype(BF16)
    return high, (x - high.astype(F32)).astype(BF16)


def dot(x, y):
    return jnp.dot(x, y, preferred_element_type=F32)


def dot_nt(x, y):
    return lax.dot_general(x, y, (((1,), (1,)), ((), ())), preferred_element_type=F32)


def times(x, pair):
    high, low = halves(x)
    return dot(high, pair[0]) + dot(low, pair[0]) + dot(high, pair[1])


def inputs_kernel(members, sign, place, obs, gain, out, held, total, sems):
    half = place[0] if sign > 0 else 1 - place[0]
    steps = obs.shape[1]
    cut = min(16, members)
    copies = []
    for i in range(members // cut):
        copy = pltpu.make_async_copy(
            obs.at[pl.ds(half * members + i * cut, cut)], held.at[pl.ds(i * cut, cut)], sems.at[i]
        )
        copy.start()
        copies.append(copy)
    rows = cut * steps
    for i, copy in enumerate(copies):
        copy.wait()
        part = held[pl.ds(i * cut, cut)].reshape(rows, obs.shape[2])
        product = dot_nt(part, gain[...])
        for j in range(total.shape[0]):
            total[j, pl.ds(i * rows, rows)] = product[:, j * LANES : (j + 1) * LANES]
    for t in range(steps):
        for j in range(total.shape[0]):
            step = total.at[j][pl.ds(t, members, stride=steps)]
            out[pl.ds(t * members, members), pl.ds(j * LANES, LANES)] = step.astype(out.dtype)


def half_inputs(place, obs, gain, members, sign, dtype):
    steps, states = obs.shape[1], gain.shape[0]

    def kernel(*refs):
        inputs_kernel(members, sign, *refs)

    rows = members * steps
    return pl.pallas_call(
        kernel,
        out_shape=jax.ShapeDtypeStruct((rows, states), dtype),
        in_specs=[SMEM, pl.BlockSpec(memory_space=pl.ANY), VMEM],
        out_specs=VMEM,
        scratch_shapes=[
            pltpu.VMEM((members, steps, obs.shape[2]), BF16),
            pltpu.VMEM((states // LANES, rows, LANES), F32),
            pltpu.SemaphoreType.DMA((max(1, members // 16),)),
        ],
        compiler_params=PARAMS,
        cost_estimate=pl.CostEstimate(
            flops=2 * rows * states * obs.shape[2], bytes_accessed=2 * rows * obs.shape[2], transcendentals=0
        ),
        name="inputs_other" if sign < 0 else "inputs_own",
    )(place, obs, gain)


def store(ref, index, value):
    high, low = halves(value)
    ref[index, 0] = high
    ref[index, 1] = low
    return high, low


def first_kernel(levels, loop, gain, transition, out, carry):
    a = loop[...].T
    g = gain[...].T
    w = dot(transition[...].T, gain[...].astype(BF16).T)
    ga = halves(g)
    b = g - times(w, ga)
    store(out, 0, w)
    ap, gp = store(out, 1, a), store(out, 2, g)
    k = times(a, halves(b))
    c = times(k, gp)
    store(out, 3, b + c)
    store(out, 4, times(b, gp))
    powers(levels, a, g, k, c, ap, gp, out, 5, carry)


def powers(levels, a, g, k, c, ap, gp, out, at, carry):
    for _ in range(levels):
        k = k + times(a, halves(c))
        a, g = times(a, ap), times(g, gp)
        c = times(k, halves(g))
        ap, gp = store(out, at, a), store(out, at + 1, g)
        store(out, at + 2, k)
        store(out, at + 3, c)
        at += 4
    for i, x in enumerate((a, g, k, c)):
        carry[i] = x


def next_kernel(levels, given, out):
    a, g, k, c = (given[i] for i in range(4))
    ap, gp = halves(a), halves(g)

    for level in range(levels):
        k = k + times(a, halves(c))
        a, g = times(a, ap), times(g, gp)
        c = times(k, halves(g))
        ap, gp = store(out, 4 * level, a), store(out, 4 * level + 1, g)
        store(out, 4 * level + 2, k)
        store(out, 4 * level + 3, c)


def first_powers(loop, gain, transition, levels):
    n = loop.shape[0]

    def kernel(*refs):
        first_kernel(levels, *refs)

    return pl.pallas_call(
        kernel,
        out_shape=(
            jax.ShapeDtypeStruct((5 + 4 * levels, 2, n, n), BF16),
            jax.ShapeDtypeStruct((4, n, n), F32),
        ),
        in_specs=[VMEM] * 3,
        out_specs=(VMEM, VMEM),
        compiler_params=PARAMS,
        cost_estimate=pl.CostEstimate(flops=2 * n**3 * 12 * levels, bytes_accessed=0, transcendentals=0),
        name="first_powers",
    )(loop, gain, transition)


def next_powers(given, levels):
    n = given.shape[1]

    def kernel(*refs):
        next_kernel(levels, *refs)

    return pl.pallas_call(
        kernel,
        out_shape=jax.ShapeDtypeStruct((4 * levels, 2, n, n), BF16),
        in_specs=[VMEM],
        out_specs=VMEM,
        compiler_params=PARAMS,
        cost_estimate=pl.CostEstimate(flops=2 * n**3 * 12 * levels, bytes_accessed=0, transcendentals=0),
        name="next_powers",
    )(given)


def pair_of(ref, index):
    return ref[index, 0], ref[index, 1]


def up_kernel(members, levels, own, other, mats, u_out, e_out, h_out, ends, payload):
    states = own.shape[1]
    u = own[...] + other[...].astype(F32)
    u_out[...] = u
    nodes = u.reshape(-1, 2, members, states)
    left = nodes[:, 0].reshape(-1, states)
    right = nodes[:, 1].reshape(-1, states)
    e = times(left, pair_of(mats, 1)) + right
    h = times(left, pair_of(mats, 3)) + times(right, pair_of(mats, 4))
    row = 0
    for level in range(levels):
        base = 5 + 4 * level
        e2 = e.reshape(-1, 2, members, states)
        h2 = h.reshape(-1, 2, members, states)
        el, er = e2[:, 0].reshape(-1, states), e2[:, 1].reshape(-1, states)
        hl, hr = h2[:, 0].reshape(-1, states), h2[:, 1].reshape(-1, states)
        count = el.shape[0]
        e_out[pl.ds(row, count)] = el
        h_out[pl.ds(row, count)] = hr
        row += count
        e = times(el, pair_of(mats, base)) + er
        h = hl + times(hr, pair_of(mats, base + 1)) + times(el, pair_of(mats, base + 3))
    ends[0] = e
    ends[1] = h
    payload[:, pl.ds(0, states)] = e.astype(BF16)
    payload[:, pl.ds(states, states)] = h.astype(BF16)


def up(own, other, mats, members, levels):
    rows, states = own.shape
    kept = members * (rows // members // 2 - 1)

    def kernel(*refs):
        up_kernel(members, levels, *refs)

    return pl.pallas_call(
        kernel,
        out_shape=(
            jax.ShapeDtypeStruct((rows, states), F32),
            jax.ShapeDtypeStruct((kept, states), F32),
            jax.ShapeDtypeStruct((kept, states), F32),
            jax.ShapeDtypeStruct((2, members, states), F32),
            jax.ShapeDtypeStruct((members, 2 * states), BF16),
        ),
        in_specs=[VMEM] * 3,
        out_specs=(VMEM,) * 5,
        compiler_params=PARAMS,
        cost_estimate=pl.CostEstimate(flops=2 * rows * states * states * 9, bytes_accessed=0, transcendentals=0),
        name="up",
    )(own, other, mats)


def sides(bit, mine, got):
    states = mine.shape[2]
    got_e = got[:, pl.ds(0, states)].astype(F32)
    got_h = got[:, pl.ds(states, states)].astype(F32)
    own_e, own_h = mine[0], mine[1]
    right = bit > 0
    el, er = jnp.where(right, got_e, own_e), jnp.where(right, own_e, got_e)
    hl, hr = jnp.where(right, got_h, own_h), jnp.where(right, own_h, got_h)
    return el, er, hl, hr


def join_kernel(level, base, bits, mine, got, mats, ends, payload):
    el, er, hl, hr = sides(bits[level], mine, got)
    states = mine.shape[2]
    e = times(el, pair_of(mats, base)) + er
    h = hl + times(hr, pair_of(mats, base + 1)) + times(el, pair_of(mats, base + 3))
    ends[0] = e
    ends[1] = h
    payload[:, pl.ds(0, states)] = e.astype(BF16)
    payload[:, pl.ds(states, states)] = h.astype(BF16)


def join(level, base, bits, mine, got, mats):
    def kernel(*refs):
        join_kernel(level, base, *refs)

    return pl.pallas_call(
        kernel,
        out_shape=(jax.ShapeDtypeStruct(mine.shape, F32), jax.ShapeDtypeStruct(got.shape, BF16)),
        in_specs=[SMEM, VMEM, VMEM, VMEM],
        out_specs=(VMEM, VMEM),
        compiler_params=PARAMS,
        cost_estimate=pl.CostEstimate(flops=2**27, bytes_accessed=0, transcendentals=0),
        name="join",
    )(bits, mine, got, mats)


def down_kernel(members, levels, groups, bits, *refs):
    begin, u_ref, e_ref, h_ref, mats, higher, transition, gain = refs[:8]
    mine = refs[8 : 8 + groups]
    got = refs[8 + groups : 8 + 2 * groups]
    filtered, smoothed, filtered_held, smoothed_held, sems = refs[8 + 2 * groups :]
    states = u_ref.shape[1]
    steps = u_ref.shape[0] // members

    def level_mats(level):
        if level < levels:
            return tuple(pair_of(mats, 5 + 4 * level + i) for i in range(3))
        return tuple(pair_of(higher, 4 * (level - levels) + i) for i in range(3))

    x = begin[...]
    d = None
    last = None
    for group in reversed(range(groups)):
        a, g, k = level_mats(levels - 1 + group + 1)
        right = bits[group] > 0
        el, er, _, hr = sides(bits[group], mine[group], got[group])
        middle = times(x, a) + el
        if d is None:
            w = pair_of(mats, 0)
            d = times(times(middle, a) + er, w)
            last = right
        else:
            last = jnp.logical_and(last, right)
        back = times(d, g) + times(middle, k) + hr
        x, d = jnp.where(right, middle, x), jnp.where(right, d, back)
    row = e_ref.shape[0]
    for level in reversed(range(levels)):
        a, g, k = level_mats(level)
        count = x.shape[0]
        row -= count
        middle = times(x, a) + e_ref[pl.ds(row, count)]
        back = times(d, g) + times(middle, k) + h_ref[pl.ds(row, count)]
        shape = (-1, 1, members, states)
        x = jnp.concatenate([x.reshape(shape), middle.reshape(shape)], 1).reshape(-1, states)
        d = jnp.concatenate([back.reshape(shape), d.reshape(shape)], 1).reshape(-1, states)
    a, g = pair_of(mats, 1), pair_of(mats, 2)
    u2 = u_ref[...].reshape(-1, 2, members, states)
    even = times(x, a) + u2[:, 0].reshape(-1, states)
    odd = times(even, a) + u2[:, 1].reshape(-1, states)
    gain_low = gain[...].astype(BF16)

    def adjusted(f):
        predicted = dot_nt(f.astype(BF16), transition[...]).astype(BF16)
        return f - dot_nt(predicted, gain_low)

    def write(held, out, sem, pair):
        copies = []
        for j in range(held.shape[0]):
            for t in range(steps):
                part = pair[t % 2][(t // 2) * members : (t // 2 + 1) * members]
                held.at[j][pl.ds(t, members, stride=steps)] = part[:, j * LANES : (j + 1) * LANES]
            copy = pltpu.make_async_copy(held.at[j], out.at[:, pl.ds(j * LANES, LANES)], sem.at[j])
            copy.start()
            copies.append(copy)
        return copies

    pairs = steps // 2
    copies = write(filtered_held, filtered, sems.at[0], (even, odd))
    s_odd = adjusted(odd) + d
    tail = (pairs - 1) * members
    final = jnp.where(last, odd[tail:], s_odd[tail:])
    s_odd = jnp.concatenate([s_odd[:tail], final], 0)
    s_even = adjusted(even) + times(s_odd, g)
    copies += write(smoothed_held, smoothed, sems.at[1], (s_even, s_odd))
    for copy in copies:
        copy.wait()


def down(bits, begin, u, es, hs, mats, higher, transition, gain, mine, got, levels):
    members, states = begin.shape
    groups = len(mine)

    def kernel(*refs):
        down_kernel(members, levels, groups, *refs)

    return pl.pallas_call(
        kernel,
        out_shape=(jax.ShapeDtypeStruct(u.shape, F32),) * 2,
        in_specs=[SMEM] + [VMEM] * (8 + 2 * groups),
        out_specs=(pl.BlockSpec(memory_space=pl.ANY),) * 2,
        scratch_shapes=[
            pltpu.VMEM((states // LANES, u.shape[0], LANES), F32),
            pltpu.VMEM((states // LANES, u.shape[0], LANES), F32),
            pltpu.SemaphoreType.DMA((2, states // LANES)),
        ],
        compiler_params=PARAMS,
        cost_estimate=pl.CostEstimate(
            flops=2 * u.shape[0] * states * states * 12, bytes_accessed=0, transcendentals=0
        ),
        name="down",
    )(bits, begin, u, es, hs, mats, higher, transition, gain, *mine, *got)


def log2(n):
    power = n.bit_length() - 1
    assert n == 1 << power
    return power


def body(observations, obs_gain, closed_loop, transition, smoother_gain, initial_mean):
    members, states = initial_mean.shape
    steps = observations.shape[1]
    levels = log2(steps) - 1
    blocks = lax.axis_size("tm")
    groups = log2(blocks)
    place = lax.axis_index("sens").astype(jnp.int32).reshape(1)
    position = lax.axis_index("tm").astype(jnp.int32)
    bits = jnp.stack([(position >> i) & 1 for i in range(groups)])

    to_send = half_inputs(place, observations, obs_gain, members, -1, BF16)
    other = lax.ppermute(to_send, "sens", [(0, 1), (1, 0)])
    own = half_inputs(place, observations, obs_gain, members, 1, F32)
    mats, carry = first_powers(closed_loop, smoother_gain, transition, levels)
    u, es, hs, ends, payload = up(own, other, mats, members, levels)
    higher = next_powers(carry, groups)
    mine, got = [], []
    for group in range(groups):
        mine.append(ends)
        arrived = lax.ppermute(payload, "tm", [(i, i ^ (1 << group)) for i in range(blocks)])
        got.append(arrived)
        if group < groups - 1:
            ends, payload = join(group, 4 * group, bits, ends, arrived, higher)
    filtered, smoothed = down(
        bits, initial_mean, u, es, hs, mats, higher, transition, smoother_gain, mine, got, levels
    )
    shape = (members, steps, states)
    return filtered.reshape(shape), smoothed.reshape(shape)


def solution(mesh):
    placed = (
        P(("rec", "state"), "tm", "sens"),
        P(None, "sens"),
        P(),
        P(),
        P(),
        P(("rec", "state", "sens"), None),
    )
    return jax.shard_map(
        body,
        mesh=mesh,
        in_specs=placed,
        out_specs=(
            P(("rec", "state", "sens"), "tm", None),
            P(("rec", "state", "sens"), "tm", None),
        ),
        check_vma=False,
    )
```

```python
import jax
import jax.numpy as jnp
from jax import lax
from jax.experimental import pallas as pl
from jax.experimental.pallas import tpu as pltpu
from jax.sharding import PartitionSpec as P

F32 = jnp.float32
BF16 = jnp.bfloat16
LANES = 128
VMEM = pl.BlockSpec(memory_space=pltpu.VMEM)
SMEM = pl.BlockSpec(memory_space=pltpu.SMEM)
ANY = pl.BlockSpec(memory_space=pl.ANY)
PARAMS = pltpu.CompilerParams(vmem_limit_bytes=24 * 2**20)


def halves(x):
    high = x.astype(BF16)
    return high, (x - high.astype(F32)).astype(BF16)


def dot(x, y):
    return jnp.dot(x, y, preferred_element_type=F32)


def dot_nt(x, y):
    return lax.dot_general(x, y, (((1,), (1,)), ((), ())), preferred_element_type=F32)


def mul(x, y):
    return muls((x, y))


def muls(*terms):
    left, right = [], []
    for x, y in terms:
        left += [x[0], x[1], x[0]]
        right += [y[0], y[0], y[1]]
    return dot(jnp.concatenate(left, 1), jnp.concatenate(right, 0))


class Both:
    def __init__(self, first, second):
        self.stacks = first, second

    def of(self, name):
        return self.stacks[0] if name in self.stacks[0].place else self.stacks[1]

    def put(self, name, value):
        return self.of(name).put(name, value)

    def __getitem__(self, name):
        return self.of(name)[name]


class Stack:
    def __init__(self, names, ref):
        self.place = {name: i for i, name in enumerate(names)}
        self.ref = ref

    def put(self, name, value):
        pair = halves(value)
        self.copy(name, pair)
        return pair

    def copy(self, name, pair):
        self.ref[self.place[name], 0] = pair[0]
        self.ref[self.place[name], 1] = pair[1]

    def __getitem__(self, name):
        return self.ref[self.place[name], 0], self.ref[self.place[name], 1]


def stack_shape(names, n):
    return jax.ShapeDtypeStruct((len(names), 2, n, n), BF16)


def cost(flops):
    return pl.CostEstimate(flops=int(flops), bytes_accessed=0, transcendentals=0)


def split_cols(held, row, product):
    rows = product.shape[0]
    for j in range(held.shape[0]):
        held[j, pl.ds(row, rows)] = product[:, j * LANES : (j + 1) * LANES]


def by_step(held, out, members, steps):
    for t in range(steps):
        for j in range(held.shape[0]):
            step = held.at[j][pl.ds(t, members, stride=steps)]
            out[pl.ds(t * members, members), pl.ds(j * LANES, LANES)] = step.astype(out.dtype)


FIRST = ("a1", "a2", "a3", "a4", "g1", "g2", "g3", "g4", "w", "b")
SECOND = ("a8", "a12", "g8", "g12", "C0", "C1", "C2", "C3", "k4", "b1", "b2")
BLOCK = ("a", "g", "k", "c", "V0", "V1", "V2", "v0", "v1", "v2")
DOUBLE = ("a", "g", "k", "c")
READY = ("Z1x", "Z1d", "Z2d")


def first_powers(packed, transition):
    n = packed.shape[2]

    def kernel(packed, tr, out):
        m = Stack(FIRST, out)
        a1 = m.put("a1", packed[0].T)
        g_full = packed[1].T
        g1 = m.put("g1", g_full)
        w = m.put("w", dot(tr[...].T, g1[0]))
        a2, g2 = m.put("a2", mul(a1, a1)), m.put("g2", mul(g1, g1))
        m.put("b", g_full - mul(w, g1))
        m.put("a3", mul(a2, a1))
        m.put("a4", mul(a2, a2))
        m.put("g3", mul(g2, g1))
        m.put("g4", mul(g2, g2))

    return pl.pallas_call(
        kernel,
        out_shape=stack_shape(FIRST, n),
        in_specs=[VMEM, VMEM],
        out_specs=VMEM,
        compiler_params=PARAMS,
        cost_estimate=cost(1e9),
        name="first_powers",
    )(packed, transition)


def second_powers(first, own, other):
    n = first.shape[2]

    def kernel(first_ref, own, other, out, u, held, sem):
        copy = pltpu.make_async_copy(other, held, sem)
        copy.start()
        f, m = Stack(FIRST, first_ref), Stack(SECOND, out)
        a1, a2, a3, a4, g4, b = (f[name] for name in ("a1", "a2", "a3", "a4", "g4", "b"))
        full, beta = [b[0].astype(F32) + b[1].astype(F32)], [b]
        for i in range(1, 4):
            full.append(mul(b, f["g%d" % i]))
            beta.append(m.put(("b1", "b2", "C3")[i - 1], full[i]))
        a8, g8 = m.put("a8", mul(a4, a4)), m.put("g8", mul(g4, g4))
        c0 = m.put("C0", full[0] + muls((a1, beta[1]), (a2, beta[2]), (a3, beta[3])))
        m.put("C1", full[1] + muls((a1, beta[2]), (a2, beta[3])))
        m.put("C2", full[2] + mul(a1, beta[3]))
        m.put("a12", mul(a8, a4))
        m.put("g12", mul(g8, g4))
        m.put("k4", mul(a1, c0))
        copy.wait()
        u[...] = own[...] + held[...].astype(F32)

    return pl.pallas_call(
        kernel,
        out_shape=(stack_shape(SECOND, n), jax.ShapeDtypeStruct(own.shape, F32)),
        in_specs=[VMEM, VMEM, ANY],
        out_specs=(VMEM, VMEM),
        scratch_shapes=[pltpu.VMEM(other.shape, BF16), pltpu.SemaphoreType.DMA],
        compiler_params=PARAMS,
        cost_estimate=cost(1.5e9),
        name="second_powers",
    )(first, own, other)


def half_inputs(place, obs, gain, members, sign, dtype):
    steps, sensors = obs.shape[1:]
    states = gain.shape[0]
    cut = 16
    rows = cut * steps

    def kernel(place, obs, gain, out, held):
        half = place[0] if sign > 0 else 1 - place[0]
        for i in range(members // cut):
            part = obs[pl.ds(half * members + i * cut, cut)].reshape(rows, sensors)
            split_cols(held, i * rows, dot_nt(part, gain[...]))
        by_step(held, out, members, steps)

    return pl.pallas_call(
        kernel,
        out_shape=jax.ShapeDtypeStruct((members * steps, states), dtype),
        in_specs=[SMEM, VMEM, VMEM],
        out_specs=VMEM,
        scratch_shapes=[pltpu.VMEM((states // LANES, members * steps, LANES), F32)],
        compiler_params=PARAMS,
        cost_estimate=cost(2 * rows * sensors * states * 4),
        name="inputs_own" if sign > 0 else "inputs_other",
    )(place, obs, gain)


def put_payload(payload, e, h):
    states = e.shape[1]
    payload[:, pl.ds(0, states)] = e.astype(BF16)
    payload[:, pl.ds(states, states)] = h.astype(BF16)


def up(u, first, second, members):
    rows, states = u.shape
    quads = rows // members // 4

    def kernel(u, first_ref, second_ref, e_out, x_out, d_out, ends, payload):
        f = s = Both(Stack(FIRST, first_ref), Stack(SECOND, second_ref))
        u = u[...].reshape(quads, 4, members, states)
        full = [u[:, j].reshape(-1, states) for j in range(4)]
        pairs = [halves(x) for x in full]
        e = full[3] + muls((pairs[2], f["a1"]), (pairs[1], f["a2"]), (pairs[0], f["a3"]))
        h = muls(*((pairs[j], s["C%d" % j]) for j in range(4)))
        e_out[...] = e
        cut = lambda x, q: x[q * members : (q + 1) * members]
        ah = [f["a4"], s["a8"], s["a12"]]
        gh = [f["g4"], s["g8"], s["g12"]]
        ep = [halves(cut(e, q)) for q in range(quads)]
        entering = [cut(e, 0)]
        for q in range(1, quads):
            entering.append(cut(e, q) + muls(*((ep[p], ah[q - p - 1]) for p in range(q))))
        x = jnp.concatenate(entering[:-1], 0)
        x_out[...] = x
        back_x = mul(halves(x), s["k4"])
        backs = [cut(h, 0)] + [cut(h, q) + cut(back_x, q - 1) for q in range(1, quads)]
        bp = [halves(x) for x in backs]
        handed = [
            backs[q] + muls(*((bp[p], gh[p - q - 1]) for p in range(q + 1, quads))) for q in range(quads - 1)
        ] + [backs[-1]]
        d_out[...] = jnp.concatenate(handed[1:], 0)
        ends[0] = entering[-1]
        ends[1] = handed[0]
        put_payload(payload, entering[-1], handed[0])

    return pl.pallas_call(
        kernel,
        out_shape=(
            jax.ShapeDtypeStruct((quads * members, states), F32),
            jax.ShapeDtypeStruct(((quads - 1) * members, states), F32),
            jax.ShapeDtypeStruct(((quads - 1) * members, states), F32),
            jax.ShapeDtypeStruct((2, members, states), F32),
            jax.ShapeDtypeStruct((members, 2 * states), BF16),
        ),
        in_specs=[VMEM] * 3,
        out_specs=(VMEM,) * 5,
        compiler_params=PARAMS,
        cost_estimate=cost(2e9),
        name="up",
    )(u, first, second)


def block_maps(mats_in, single, after):
    n = mats_in.shape[2]

    def kernel(mats_ref, single_ref, _, out):
        f = s = Both(Stack(FIRST, mats_ref), Stack(SECOND, single_ref))
        mats = Stack(BLOCK, out)
        k4, a4, g4, a8, g8 = s["k4"], f["a4"], f["g4"], s["a8"], s["g8"]
        full = [mul(x, k4) for x in (a4, a8, s["a12"])]
        t = [halves(x) for x in full]
        mats.put("a", mul(a8, a8))
        g = mats.put("g", mul(g8, g8))
        k = k4[0].astype(F32) + k4[1].astype(F32)
        k = mats.put("k", k + muls((t[0], g4), (t[1], g8), (t[2], s["g12"])))
        mats.put("V0", full[0] + muls((t[1], g4), (t[2], g8)))
        mats.put("V1", full[1] + mul(t[2], g4))
        mats.copy("V2", t[2])
        mats.put("c", mul(k, g))
        b, b1, b2, a2, a3 = f["b"], f["b1"], f["b2"], f["a2"], f["a3"]
        mats.put("v2", mul(a4, b))
        mats.put("v1", muls((a3, b), (a4, b1)))
        mats.put("v0", muls((a2, b), (a3, b1), (a4, b2)))

    return pl.pallas_call(
        kernel,
        out_shape=stack_shape(BLOCK, n),
        in_specs=[VMEM, VMEM, ANY],
        out_specs=VMEM,
        compiler_params=PARAMS,
        cost_estimate=cost(1.2e9),
        name="block_maps",
    )(mats_in, single, after)


def double_maps(names, given, last):
    n = given.shape[2]
    kept = DOUBLE[:3] if last else DOUBLE

    def kernel(given_ref, out):
        s = Stack(names, given_ref)
        mats = Stack(kept, out)
        a, g, k = s["a"], s["g"], s["k"]
        mats.put("a", mul(a, a))
        g = mats.put("g", mul(g, g))
        k = mats.put("k", k[0].astype(F32) + k[1].astype(F32) + mul(a, s["c"]))
        if not last:
            mats.put("c", mul(k, g))

    return pl.pallas_call(
        kernel,
        out_shape=stack_shape(kept, n),
        in_specs=[VMEM],
        out_specs=VMEM,
        compiler_params=PARAMS,
        cost_estimate=cost(4e8),
        name="double_maps",
    )(given)


def sides(bit, mine, got):
    states = mine.shape[2]
    got_e = got[:, pl.ds(0, states)].astype(F32)
    got_h = got[:, pl.ds(states, states)].astype(F32)
    right = bit > 0
    el, er = jnp.where(right, got_e, mine[0]), jnp.where(right, mine[0], got_e)
    hl, hr = jnp.where(right, got_h, mine[1]), jnp.where(right, mine[1], got_h)
    return el, er, hl, hr


def join(level, names, bits, mine, got, mats):
    def kernel(bits, mine, got, mats_ref, ends, payload):
        m = Stack(names, mats_ref)
        el, er, hl, hr = sides(bits[level], mine, got)
        pair = halves(el)
        e = mul(pair, m["a"]) + er
        h = hl + muls((halves(hr), m["g"]), (pair, m["c"]))
        ends[0] = e
        ends[1] = h
        put_payload(payload, e, h)

    return pl.pallas_call(
        kernel,
        out_shape=(jax.ShapeDtypeStruct(mine.shape, F32), jax.ShapeDtypeStruct(got.shape, BF16)),
        in_specs=[SMEM, VMEM, VMEM, VMEM],
        out_specs=(VMEM, VMEM),
        compiler_params=PARAMS,
        cost_estimate=cost(1e8),
        name="join",
    )(bits, mine, got, mats)


def either(flag, x, y):
    return tuple(jnp.where(flag, p, q) for p, q in zip(x, y, strict=True))


def ready(bits, begin, u, e_groups, mats_in, single, maps, ends, got):
    members, states = begin.shape
    rows = u.shape[0]
    quads = rows // members // 4
    top = len(maps) - 1

    def kernel(bits, begin, u, e_groups, mats_ref, single_ref, *refs):
        f = Both(Stack(FIRST, mats_ref), Stack(SECOND, single_ref))
        level_maps = [Stack(BLOCK if i == 0 else DOUBLE, refs[i]) for i in range(top + 1)]
        mine = refs[top + 1 : 2 * top + 2]
        arrived = refs[2 * top + 2 : 3 * top + 2]
        out_ref, pre, local, local_d = refs[3 * top + 2 :]
        mats = Stack(READY, out_ref)
        unit = halves(jnp.eye(states, dtype=F32))
        none = tuple(jnp.zeros_like(x) for x in unit)
        zero = jnp.zeros((members, states), F32)
        p, q, r, px, pd = unit, unit, none, zero, zero
        for i in range(top):
            m = level_maps[i]
            right = bits[i] > 0
            el, _, _, hr = sides(bits[i], mine[i], arrived[i])
            elp = halves(el)
            hand = mul(elp, m["k"]) + hr
            ak = halves(mul(m["a"], m["k"]))
            if i == 0:
                p, q, r = either(right, m["a"], unit), either(right, unit, m["g"]), either(right, none, ak)
                px, pd = jnp.where(right, el, zero), jnp.where(right, zero, hand)
            else:
                px, pd = (
                    jnp.where(right, mul(elp, p) + px, px),
                    jnp.where(right, mul(elp, r) + pd, mul(halves(hand), q) + pd),
                )
                r = either(
                    right,
                    halves(mul(m["a"], r)),
                    halves(mul(ak, q) + r[0].astype(F32) + r[1].astype(F32)),
                )
                p, q = either(right, halves(mul(m["a"], p)), p), either(right, q, halves(mul(m["g"], q)))
        m = level_maps[top]
        right = bits[top] > 0
        w = f["w"]
        x0 = begin[...]
        own_e = mine[top][0]
        aw = halves(mul(m["a"], w))
        wg = halves(mul(w, m["g"]))
        middle = mul(halves(x0), m["a"]) + jnp.where(right, zero, own_e)
        middle_p = halves(middle)
        far = halves(mul(aw, m["g"]) + m["k"][0].astype(F32) + m["k"][1].astype(F32))
        x_in = jnp.where(right, middle, x0)
        d_in = mul(middle_p, either(right, aw, far)) + jnp.where(right, mul(halves(own_e), w), zero)
        x_in_p = halves(x_in)
        pre[0] = mul(x_in_p, p) + px
        pre[1] = muls((halves(d_in), q), (x_in_p, r)) + pd
        mats.copy("Z1x", either(right, p, none))
        after = mul(either(right, aw, wg), q)
        after_r = r[0].astype(F32) + r[1].astype(F32)
        mats.put("Z1d", jnp.where(right, after + after_r, after))
        mats.copy("Z2d", either(right, none, q))
        b, b1, b2 = f["b"], f["b1"], f["b2"]
        v = u[...].reshape(quads, 4, members, states)
        part = [v[:, j].reshape(-1, states) for j in range(3)]
        pairs = [halves(x) for x in part[:2]]
        f1 = part[1] + mul(pairs[0], f["a1"])
        f2 = part[2] + muls((pairs[1], f["a1"]), (pairs[0], f["a2"]))
        local[0], local[1], local[2], local[3] = part[0], f1, f2, e_groups[...]
        p1, p2, p3 = halves(f1), halves(f2), halves(e_groups[...])
        local_d[2] = mul(p3, b)
        local_d[1] = muls((p2, b), (p3, b1))
        local_d[0] = muls((p1, b), (p2, b1), (p3, b2))

    return pl.pallas_call(
        kernel,
        out_shape=(
            stack_shape(READY, states),
            jax.ShapeDtypeStruct((2, members, states), F32),
            jax.ShapeDtypeStruct((4, quads * members, states), F32),
            jax.ShapeDtypeStruct((3, quads * members, states), F32),
        ),
        in_specs=[SMEM] + [VMEM] * (5 + len(maps) + len(ends) + len(got)),
        out_specs=(VMEM,) * 4,
        compiler_params=PARAMS,
        cost_estimate=cost(3e9),
        name="ready",
    )(bits, begin, u, e_groups, mats_in, single, *maps, *ends, *got)


def finish(bits, got, prepared, pre, local, local_d, x_groups, d_groups, mats, single, block, transition, gain):
    members, states = pre.shape[1:]
    quads = local.shape[1] // members
    steps = 4 * quads
    groups = bits.shape[0]

    def kernel(bits, got, ready_ref, pre, local, local_d, xg, dg, mats_ref, single_ref, block_ref, tr, ga, *refs):
        filtered, smoothed, filtered_held, smoothed_held, sems = refs
        z, m = Stack(READY, ready_ref), Stack(BLOCK, block_ref)
        f = s = Both(Stack(FIRST, mats_ref), Stack(SECOND, single_ref))
        e, h = got[:, pl.ds(0, states)], got[:, pl.ds(states, states)]
        exact = lambda x, y: dot(x, y[0]) + dot(x, y[1])
        x = exact(e, z["Z1x"]) + pre[0]
        d = exact(e, z["Z1d"]) + exact(h, z["Z2d"]) + pre[1]
        xp, dp = halves(x), halves(d)
        ah, gh = [f["a4"], s["a8"], s["a12"]], [f["g4"], s["g8"], s["g12"]]
        xs, ds = [x], []
        for q in range(1, quads):
            part = pl.ds((q - 1) * members, members)
            xs.append(xg[part] + mul(xp, ah[q - 1]))
            ds.append(dg[part] + muls((dp, gh[quads - q - 1]), (xp, m["V%d" % (q - 1)])))
        x = jnp.concatenate(xs, 0)
        d = jnp.concatenate(ds + [d], 0)
        xp, dp = halves(x), halves(d)
        low = ga[...].astype(BF16)
        final = bits[0] > 0
        for i in range(1, groups):
            final = jnp.logical_and(final, bits[i] > 0)

        def write(held, j, value):
            for q in range(quads):
                for c in range(held.shape[0]):
                    piece = value[q * members : (q + 1) * members, c * LANES : (c + 1) * LANES]
                    held.at[c][pl.ds(4 * q + j, members, stride=steps)] = piece

        def send(held, out, sem):
            copies = []
            for c in range(held.shape[0]):
                copies.append(pltpu.make_async_copy(held.at[c], out.at[:, pl.ds(c * LANES, LANES)], sem.at[c]))
                copies[-1].start()
            return copies

        states_of = []
        for j in range(4):
            value = local[j] + mul(xp, f["a%d" % (j + 1)])
            states_of.append(value)
            write(filtered_held, j, value)
        copies = send(filtered_held, filtered, sems.at[0])
        for j in range(4):
            value = states_of[j]
            if j < 3:
                handed = local_d[j] + muls((dp, f["g%d" % (3 - j)]), (xp, m["v%d" % j]))
            else:
                handed = d
            predicted = dot_nt(value.astype(BF16), tr[...]).astype(BF16)
            result = value - dot_nt(predicted, low) + handed
            if j == 3:
                tail = (quads - 1) * members
                result = jnp.concatenate([result[:tail], jnp.where(final, value[tail:], result[tail:])], 0)
            write(smoothed_held, j, result)
        copies += send(smoothed_held, smoothed, sems.at[1])
        for copy in copies:
            copy.wait()

    return pl.pallas_call(
        kernel,
        out_shape=(jax.ShapeDtypeStruct((members * steps, states), F32),) * 2,
        in_specs=[SMEM] + [VMEM] * 12,
        out_specs=(ANY,) * 2,
        scratch_shapes=[
            pltpu.VMEM((states // LANES, members * steps, LANES), F32),
            pltpu.VMEM((states // LANES, members * steps, LANES), F32),
            pltpu.SemaphoreType.DMA((2, states // LANES)),
        ],
        compiler_params=PARAMS,
        cost_estimate=cost(3e9),
        name="finish",
    )(bits, got, prepared, pre, local, local_d, x_groups, d_groups, mats, single, block, transition, gain)


def body(observations, obs_gain, closed_loop, transition, smoother_gain, initial_mean):
    members, states = initial_mean.shape
    steps = observations.shape[1]
    assert steps == 16
    blocks = lax.axis_size("tm")
    groups = blocks.bit_length() - 1
    assert blocks == 1 << groups
    place = lax.axis_index("sens").astype(jnp.int32).reshape(1)
    position = lax.axis_index("tm").astype(jnp.int32)
    bits = jnp.stack([(position >> i) & 1 for i in range(groups)])

    packed = jnp.stack([closed_loop, smoother_gain])
    to_send = half_inputs(place, observations, obs_gain, members, -1, BF16)
    other = lax.ppermute(to_send, "sens", [(0, 1), (1, 0)])
    own = half_inputs(place, observations, obs_gain, members, 1, F32)
    mats = first_powers(packed, transition)
    single, u = second_powers(mats, own, other)
    e_groups, x_groups, d_groups, ends, payload = up(u, mats, single, members)
    block = block_maps(mats, single, ends)
    maps = [block]
    for i in range(1, groups):
        maps.append(double_maps(BLOCK if i == 1 else DOUBLE, maps[-1], i == groups - 1))
    mine, got = [ends], []
    for i in range(groups):
        arrived = lax.ppermute(payload, "tm", [(j, j ^ (1 << i)) for j in range(blocks)])
        got.append(arrived)
        if i < groups - 1:
            ends, payload = join(i, BLOCK if i == 0 else DOUBLE, bits, ends, arrived, maps[i])
            mine.append(ends)
    prepared, pre, local, local_d = ready(
        bits, initial_mean, u, e_groups, mats, single, maps, mine, got[:-1]
    )
    filtered, smoothed = finish(
        bits, got[-1], prepared, pre, local, local_d, x_groups, d_groups, mats, single, block, transition, smoother_gain
    )
    shape = (members, steps, states)
    return filtered.reshape(shape), smoothed.reshape(shape)


def solution(mesh):
    placed = (
        P(("rec", "state"), "tm", "sens"),
        P(None, "sens"),
        P(),
        P(),
        P(),
        P(("rec", "state", "sens"), None),
    )
    return jax.shard_map(
        body,
        mesh=mesh,
        in_specs=placed,
        out_specs=(
            P(("rec", "state", "sens"), "tm", None),
            P(("rec", "state", "sens"), "tm", None),
        ),
        check_vma=False,
    )
```

```python
import jax
import jax.numpy as jnp
from jax import lax
from jax.experimental import pallas as pl
from jax.experimental.pallas import tpu as pltpu
from jax.sharding import PartitionSpec as P

F32 = jnp.float32
BF16 = jnp.bfloat16
LANES = 128
VMEM = pl.BlockSpec(memory_space=pltpu.VMEM)
SMEM = pl.BlockSpec(memory_space=pltpu.SMEM)
ANY = pl.BlockSpec(memory_space=pl.ANY)
PARAMS = pltpu.CompilerParams(vmem_limit_bytes=24 * 2**20)


def halves(x):
    high = x.astype(BF16)
    return high, (x - high.astype(F32)).astype(BF16)


def dot(x, y):
    return jnp.dot(x, y, preferred_element_type=F32)


def dot_nt(x, y):
    return lax.dot_general(x, y, (((1,), (1,)), ((), ())), preferred_element_type=F32)


def mul(x, y):
    return muls((x, y))


def muls(*terms):
    left, right = [], []
    for x, y in terms:
        left += [x[0], x[1], x[0]]
        right += [y[0], y[0], y[1]]
    return dot(jnp.concatenate(left, 1), jnp.concatenate(right, 0))


class Both:
    def __init__(self, first, second):
        self.stacks = first, second

    def of(self, name):
        return self.stacks[0] if name in self.stacks[0].place else self.stacks[1]

    def put(self, name, value):
        return self.of(name).put(name, value)

    def __getitem__(self, name):
        return self.of(name)[name]


class Stack:
    def __init__(self, names, ref):
        self.place = {name: i for i, name in enumerate(names)}
        self.ref = ref

    def put(self, name, value):
        pair = halves(value)
        self.copy(name, pair)
        return pair

    def copy(self, name, pair):
        self.ref[self.place[name], 0] = pair[0]
        self.ref[self.place[name], 1] = pair[1]

    def __getitem__(self, name):
        return self.ref[self.place[name], 0], self.ref[self.place[name], 1]


def stack_shape(names, n):
    return jax.ShapeDtypeStruct((len(names), 2, n, n), BF16)


def cost(flops):
    return pl.CostEstimate(flops=int(flops), bytes_accessed=0, transcendentals=0)


def split_cols(held, row, product):
    rows = product.shape[0]
    for j in range(held.shape[0]):
        held[j, pl.ds(row, rows)] = product[:, j * LANES : (j + 1) * LANES]


def by_step(held, out, members, steps):
    for t in range(steps):
        for j in range(held.shape[0]):
            step = held.at[j][pl.ds(t, members, stride=steps)]
            out[pl.ds(t * members, members), pl.ds(j * LANES, LANES)] = step.astype(out.dtype)


FIRST = ("a1", "a2", "a3", "a4", "g1", "g2", "g3", "g4", "w", "b")
SECOND = ("a8", "a12", "g8", "g12", "C0", "C1", "C2", "C3", "k4")
BLOCK = ("a", "g", "k", "c", "V0", "V1", "V2")
DOUBLE = ("a", "g", "k", "c")
TOP = ("a", "g", "k", "wg", "c2")
READY = ("Zx", "Zd")


def first_powers(packed, transition):
    n = packed.shape[2]

    def kernel(packed, tr, out):
        m = Stack(FIRST, out)
        a1 = m.put("a1", packed[0].T)
        g_full = packed[1].T
        g1 = m.put("g1", g_full)
        w = m.put("w", dot(tr[...].T, g1[0]))
        a2, g2 = m.put("a2", mul(a1, a1)), m.put("g2", mul(g1, g1))
        m.put("b", g_full - mul(w, g1))
        m.put("a3", mul(a2, a1))
        m.put("a4", mul(a2, a2))
        m.put("g3", mul(g2, g1))
        m.put("g4", mul(g2, g2))

    return pl.pallas_call(
        kernel,
        out_shape=stack_shape(FIRST, n),
        in_specs=[VMEM, VMEM],
        out_specs=VMEM,
        compiler_params=PARAMS,
        cost_estimate=cost(1e9),
        name="first_powers",
    )(packed, transition)


def second_powers(first, own, other):
    n = first.shape[2]

    def kernel(first_ref, own, other, out, u, held, sem):
        copy = pltpu.make_async_copy(other, held, sem)
        copy.start()
        f, m = Stack(FIRST, first_ref), Stack(SECOND, out)
        a1, a2, a3, a4, g4, b = (f[name] for name in ("a1", "a2", "a3", "a4", "g4", "b"))
        full, beta = [b[0].astype(F32) + b[1].astype(F32)], [b]
        for i in range(1, 4):
            full.append(mul(b, f["g%d" % i]))
            beta.append(m.put("C3", full[i]) if i == 3 else halves(full[i]))
        a8, g8 = m.put("a8", mul(a4, a4)), m.put("g8", mul(g4, g4))
        c0 = m.put("C0", full[0] + muls((a1, beta[1]), (a2, beta[2]), (a3, beta[3])))
        m.put("C1", full[1] + muls((a1, beta[2]), (a2, beta[3])))
        m.put("C2", full[2] + mul(a1, beta[3]))
        m.put("a12", mul(a8, a4))
        m.put("g12", mul(g8, g4))
        m.put("k4", mul(a1, c0))
        copy.wait()
        u[...] = own[...] + held[...].astype(F32)

    return pl.pallas_call(
        kernel,
        out_shape=(stack_shape(SECOND, n), jax.ShapeDtypeStruct(own.shape, F32)),
        in_specs=[VMEM, VMEM, ANY],
        out_specs=(VMEM, VMEM),
        scratch_shapes=[pltpu.VMEM(other.shape, BF16), pltpu.SemaphoreType.DMA],
        compiler_params=PARAMS,
        cost_estimate=cost(1.5e9),
        name="second_powers",
    )(first, own, other)


def half_inputs(place, obs, gain, members, sign, dtype):
    steps, sensors = obs.shape[1:]
    states = gain.shape[0]
    cut = 16
    rows = cut * steps

    def kernel(place, obs, gain, out, held):
        half = place[0] if sign > 0 else 1 - place[0]
        for i in range(members // cut):
            part = obs[pl.ds(half * members + i * cut, cut)].reshape(rows, sensors)
            split_cols(held, i * rows, dot_nt(part, gain[...]))
        by_step(held, out, members, steps)

    return pl.pallas_call(
        kernel,
        out_shape=jax.ShapeDtypeStruct((members * steps, states), dtype),
        in_specs=[SMEM, VMEM, VMEM],
        out_specs=VMEM,
        scratch_shapes=[pltpu.VMEM((states // LANES, members * steps, LANES), F32)],
        compiler_params=PARAMS,
        cost_estimate=cost(2 * rows * sensors * states * 4),
        name="inputs_own" if sign > 0 else "inputs_other",
    )(place, obs, gain)


def put_payload(payload, e, h):
    states = e.shape[1]
    payload[:, pl.ds(0, states)] = e.astype(BF16)
    payload[:, pl.ds(states, states)] = h.astype(BF16)


def up(u, first, second, members):
    rows, states = u.shape
    quads = rows // members // 4

    def kernel(u, first_ref, second_ref, e_out, x_out, d_out, ends, payload):
        f = s = Both(Stack(FIRST, first_ref), Stack(SECOND, second_ref))
        u = u[...].reshape(quads, 4, members, states)
        full = [u[:, j].reshape(-1, states) for j in range(4)]
        pairs = [halves(x) for x in full]
        e = full[3] + muls((pairs[2], f["a1"]), (pairs[1], f["a2"]), (pairs[0], f["a3"]))
        h = muls(*((pairs[j], s["C%d" % j]) for j in range(4)))
        e_out[...] = e
        cut = lambda x, q: x[q * members : (q + 1) * members]
        ah = [f["a4"], s["a8"], s["a12"]]
        gh = [f["g4"], s["g8"], s["g12"]]
        ep = [halves(cut(e, q)) for q in range(quads)]
        entering = [cut(e, 0)]
        for q in range(1, quads):
            entering.append(cut(e, q) + muls(*((ep[p], ah[q - p - 1]) for p in range(q))))
        x = jnp.concatenate(entering[:-1], 0)
        x_out[...] = x
        back_x = mul(halves(x), s["k4"])
        backs = [cut(h, 0)] + [cut(h, q) + cut(back_x, q - 1) for q in range(1, quads)]
        bp = [halves(x) for x in backs]
        handed = [
            backs[q] + muls(*((bp[p], gh[p - q - 1]) for p in range(q + 1, quads))) for q in range(quads - 1)
        ] + [backs[-1]]
        d_out[...] = jnp.concatenate(handed[1:], 0)
        ends[0] = entering[-1]
        ends[1] = handed[0]
        put_payload(payload, entering[-1], handed[0])

    return pl.pallas_call(
        kernel,
        out_shape=(
            jax.ShapeDtypeStruct((quads * members, states), F32),
            jax.ShapeDtypeStruct(((quads - 1) * members, states), F32),
            jax.ShapeDtypeStruct(((quads - 1) * members, states), F32),
            jax.ShapeDtypeStruct((2, members, states), F32),
            jax.ShapeDtypeStruct((members, 2 * states), BF16),
        ),
        in_specs=[VMEM] * 3,
        out_specs=(VMEM,) * 5,
        compiler_params=PARAMS,
        cost_estimate=cost(2e9),
        name="up",
    )(u, first, second)


def fill_block(f, mats):
    k4, a4, g4, a8, g8 = f["k4"], f["a4"], f["g4"], f["a8"], f["g8"]
    full = [mul(x, k4) for x in (a4, a8, f["a12"])]
    t = [halves(x) for x in full]
    mats.put("a", mul(a8, a8))
    g = mats.put("g", mul(g8, g8))
    k = k4[0].astype(F32) + k4[1].astype(F32)
    k = mats.put("k", k + muls((t[0], g4), (t[1], g8), (t[2], f["g12"])))
    mats.put("V0", full[0] + muls((t[1], g4), (t[2], g8)))
    mats.put("V1", full[1] + mul(t[2], g4))
    mats.copy("V2", t[2])
    mats.put("c", mul(k, g))


def fill_double(w, s, mats, top):
    a, g, k, c = s["a"], s["g"], s["k"], s["c"]
    mats.put("a", mul(a, a))
    g = mats.put("g", mul(g, g))
    k2 = mats.put("k", k[0].astype(F32) + k[1].astype(F32) + mul(a, c))
    if top:
        wg = mats.put("wg", mul(w, g))
        mats.put("c2", c[0].astype(F32) + c[1].astype(F32) + mul(a, wg))
    else:
        mats.put("c", mul(k2, g))


def all_maps(first, second, after, groups):
    n = first.shape[2]
    names = [BLOCK] + [DOUBLE] * (groups - 2) + [TOP]

    def kernel(first_ref, second_ref, _, block):
        f = Both(Stack(FIRST, first_ref), Stack(SECOND, second_ref))
        m = Stack(BLOCK, block)
        fill_block(f, m)

    def both_kernel(first_ref, second_ref, _, block, top):
        f = Both(Stack(FIRST, first_ref), Stack(SECOND, second_ref))
        m = Stack(BLOCK, block)
        fill_block(f, m)
        fill_double(f["w"], m, Stack(TOP, top), True)

    joined = groups == 2
    shapes = [stack_shape(names[i], n) for i in range(2 if joined else 1)]
    maps = pl.pallas_call(
        both_kernel if joined else kernel,
        out_shape=shapes,
        in_specs=[VMEM, VMEM, ANY],
        out_specs=[VMEM] * len(shapes),
        compiler_params=PARAMS,
        cost_estimate=cost(1.2e9),
        name="block_maps",
    )(first, second, after)
    maps = list(maps)
    while len(maps) < groups:
        maps.append(double_maps(names[len(maps) - 1], maps[-1], first, len(maps) == groups - 1))
    return maps


def double_maps(names, given, first, top):
    n = given.shape[2]
    kept = TOP if top else DOUBLE

    def kernel(given_ref, first_ref, out):
        fill_double(Stack(FIRST, first_ref)["w"], Stack(names, given_ref), Stack(kept, out), top)

    return pl.pallas_call(
        kernel,
        out_shape=stack_shape(kept, n),
        in_specs=[VMEM] * 2,
        out_specs=VMEM,
        compiler_params=PARAMS,
        cost_estimate=cost(4e8),
        name="double_maps",
    )(given, first)


def sides(bit, mine, got):
    states = mine.shape[2]
    got_e = got[:, pl.ds(0, states)].astype(F32)
    got_h = got[:, pl.ds(states, states)].astype(F32)
    right = bit > 0
    el, er = jnp.where(right, got_e, mine[0]), jnp.where(right, mine[0], got_e)
    hl, hr = jnp.where(right, got_h, mine[1]), jnp.where(right, mine[1], got_h)
    return el, er, hl, hr


def join(level, names, bits, mine, got, mats):
    def kernel(bits, mine, got, mats_ref, ends, payload):
        m = Stack(names, mats_ref)
        el, er, hl, hr = sides(bits[level], mine, got)
        pair = halves(el)
        e = mul(pair, m["a"]) + er
        h = hl + muls((halves(hr), m["g"]), (pair, m["c"]))
        ends[0] = e
        ends[1] = h
        put_payload(payload, e, h)

    return pl.pallas_call(
        kernel,
        out_shape=(jax.ShapeDtypeStruct(mine.shape, F32), jax.ShapeDtypeStruct(got.shape, BF16)),
        in_specs=[SMEM, VMEM, VMEM, VMEM],
        out_specs=(VMEM, VMEM),
        compiler_params=PARAMS,
        cost_estimate=cost(1e8),
        name="join",
    )(bits, mine, got, mats)


def last_join(level, names, bits, mine, got, mats, top_mats):
    members, states = mine.shape[1:]

    def kernel(bits, mine, got, mats_ref, top_ref, end, payload):
        m, t = Stack(names, mats_ref), Stack(TOP, top_ref)
        el, er, hl, hr = sides(bits[level], mine, got)
        pair = halves(el)
        e = er + mul(pair, m["a"])
        handed = hl + muls((halves(hr), m["g"]), (pair, t["c2"]), (halves(er), t["wg"]))
        end[0] = e
        payload[...] = jnp.where(bits[level + 1] > 0, handed, e).astype(BF16)

    return pl.pallas_call(
        kernel,
        out_shape=(
            jax.ShapeDtypeStruct((1, members, states), F32),
            jax.ShapeDtypeStruct((members, states), BF16),
        ),
        in_specs=[SMEM] + [VMEM] * 4,
        out_specs=(VMEM, VMEM),
        compiler_params=PARAMS,
        cost_estimate=cost(1e8),
        name="last_join",
    )(bits, mine, got, mats, top_mats)


def either(flag, x, y):
    return tuple(jnp.where(flag, p, q) for p, q in zip(x, y, strict=True))


def ready(bits, begin, u, e_groups, mats_in, single, maps, ends, got):
    members, states = begin.shape
    rows = u.shape[0]
    quads = rows // members // 4
    top = len(maps) - 1

    def kernel(bits, begin, u, e_groups, mats_ref, single_ref, *refs):
        f = Both(Stack(FIRST, mats_ref), Stack(SECOND, single_ref))
        level_maps = [Stack(BLOCK if i == 0 else TOP if i == top else DOUBLE, refs[i]) for i in range(top + 1)]
        mine = refs[top + 1 : 2 * top + 2]
        arrived = refs[2 * top + 2 : 3 * top + 2]
        out_ref, pre, local = refs[3 * top + 2 :]
        mats = Stack(READY, out_ref)
        unit = halves(jnp.eye(states, dtype=F32))
        none = tuple(jnp.zeros_like(x) for x in unit)
        zero = jnp.zeros((members, states), F32)
        p, q, r, px, pd = unit, unit, none, zero, zero
        for i in range(top):
            m = level_maps[i]
            right = bits[i] > 0
            el, _, _, hr = sides(bits[i], mine[i], arrived[i])
            elp = halves(el)
            hand = mul(elp, m["k"]) + hr
            ak = halves(mul(m["a"], m["k"]))
            if i == 0:
                p, q, r = either(right, m["a"], unit), either(right, unit, m["g"]), either(right, none, ak)
                px, pd = jnp.where(right, el, zero), jnp.where(right, zero, hand)
            else:
                px, pd = (
                    jnp.where(right, mul(elp, p) + px, px),
                    jnp.where(right, mul(elp, r) + pd, mul(halves(hand), q) + pd),
                )
                r = either(
                    right,
                    halves(mul(m["a"], r)),
                    halves(mul(ak, q) + r[0].astype(F32) + r[1].astype(F32)),
                )
                p, q = either(right, halves(mul(m["a"], p)), p), either(right, q, halves(mul(m["g"], q)))
        m = level_maps[top]
        right = bits[top] > 0
        w = f["w"]
        x0 = begin[...]
        own_e = mine[top][0]
        aw = halves(mul(m["a"], w))
        middle = mul(halves(x0), m["a"]) + jnp.where(right, zero, own_e)
        middle_p = halves(middle)
        far = halves(mul(aw, m["g"]) + m["k"][0].astype(F32) + m["k"][1].astype(F32))
        x_in = jnp.where(right, middle, x0)
        d_in = mul(middle_p, either(right, aw, far)) + jnp.where(right, mul(halves(own_e), w), zero)
        x_in_p = halves(x_in)
        pre[0] = mul(x_in_p, p) + px
        pre[1] = muls((halves(d_in), q), (x_in_p, r)) + pd
        mats.copy("Zx", either(right, p, none))
        near = halves(mul(aw, q) + r[0].astype(F32) + r[1].astype(F32))
        mats.copy("Zd", either(right, near, q))
        v = u[...].reshape(quads, 4, members, states)
        part = [v[:, j].reshape(-1, states) for j in range(3)]
        pairs = [halves(x) for x in part[:2]]
        local[0] = part[0]
        local[1] = part[1] + mul(pairs[0], f["a1"])
        local[2] = part[2] + muls((pairs[1], f["a1"]), (pairs[0], f["a2"]))
        local[3] = e_groups[...]

    return pl.pallas_call(
        kernel,
        out_shape=(
            stack_shape(READY, states),
            jax.ShapeDtypeStruct((2, members, states), F32),
            jax.ShapeDtypeStruct((4, quads * members, states), F32),
        ),
        in_specs=[SMEM] + [VMEM] * (5 + len(maps) + len(ends) + len(got)),
        out_specs=(VMEM,) * 3,
        compiler_params=PARAMS,
        cost_estimate=cost(3e9),
        name="ready",
    )(bits, begin, u, e_groups, mats_in, single, *maps, *ends, *got)


def finish(bits, got, prepared, pre, local, x_groups, d_groups, mats, single, block, transition, gain):
    members, states = pre.shape[1:]
    quads = local.shape[1] // members
    steps = 4 * quads
    groups = bits.shape[0]

    def kernel(bits, got, ready_ref, pre, local, xg, dg, mats_ref, single_ref, block_ref, tr, ga, *refs):
        filtered, smoothed, filtered_held, smoothed_held, sems = refs
        z, m = Stack(READY, ready_ref), Stack(BLOCK, block_ref)
        f = s = Both(Stack(FIRST, mats_ref), Stack(SECOND, single_ref))
        arrived = got[...]
        exact = lambda x, y: dot(jnp.concatenate([x, x], 1), jnp.concatenate([y[0], y[1]], 0))
        x = exact(arrived, z["Zx"]) + pre[0]
        d = exact(arrived, z["Zd"]) + pre[1]
        xp, dp = halves(x), halves(d)
        ah, gh = [f["a4"], s["a8"], s["a12"]], [f["g4"], s["g8"], s["g12"]]
        xs, ds = [x], []
        for q in range(1, quads):
            part = pl.ds((q - 1) * members, members)
            xs.append(xg[part] + mul(xp, ah[q - 1]))
            ds.append(dg[part] + muls((dp, gh[quads - q - 1]), (xp, m["V%d" % (q - 1)])))
        x = jnp.concatenate(xs, 0)
        d = jnp.concatenate(ds + [d], 0)
        xp = halves(x)
        low = ga[...].astype(BF16)
        final = bits[0] > 0
        for i in range(1, groups):
            final = jnp.logical_and(final, bits[i] > 0)

        def write(held, j, value):
            for q in range(quads):
                for c in range(held.shape[0]):
                    piece = value[q * members : (q + 1) * members, c * LANES : (c + 1) * LANES]
                    held.at[c][pl.ds(4 * q + j, members, stride=steps)] = piece

        def send(held, out, sem):
            copies = []
            for c in range(held.shape[0]):
                copies.append(pltpu.make_async_copy(held.at[c], out.at[:, pl.ds(c * LANES, LANES)], sem.at[c]))
                copies[-1].start()
            return copies

        states_of = []
        for j in range(4):
            value = local[j] + mul(xp, f["a%d" % (j + 1)])
            states_of.append(value)
            write(filtered_held, j, value)
        copies = send(filtered_held, filtered, sems.at[0])
        adjusted = []
        for j in range(4):
            predicted = dot_nt(states_of[j].astype(BF16), tr[...]).astype(BF16)
            adjusted.append(states_of[j] - dot_nt(predicted, low))
        result = adjusted[3] + d
        tail = (quads - 1) * members
        result = jnp.concatenate([result[:tail], jnp.where(final, states_of[3][tail:], result[tail:])], 0)
        write(smoothed_held, 3, result)
        later = [halves(adjusted[1]), halves(adjusted[2]), halves(result)]
        for j in range(3):
            handed = muls(*((later[i - 1], f["g%d" % (i - j)]) for i in range(j + 1, 4)))
            write(smoothed_held, j, adjusted[j] + handed)
        copies += send(smoothed_held, smoothed, sems.at[1])
        for copy in copies:
            copy.wait()

    return pl.pallas_call(
        kernel,
        out_shape=(jax.ShapeDtypeStruct((members * steps, states), F32),) * 2,
        in_specs=[SMEM] + [VMEM] * 11,
        out_specs=(ANY,) * 2,
        scratch_shapes=[
            pltpu.VMEM((states // LANES, members * steps, LANES), F32),
            pltpu.VMEM((states // LANES, members * steps, LANES), F32),
            pltpu.SemaphoreType.DMA((2, states // LANES)),
        ],
        compiler_params=PARAMS,
        cost_estimate=cost(3e9),
        name="finish",
    )(bits, got, prepared, pre, local, x_groups, d_groups, mats, single, block, transition, gain)


def body(observations, obs_gain, closed_loop, transition, smoother_gain, initial_mean):
    members, states = initial_mean.shape
    steps = observations.shape[1]
    assert steps == 16
    blocks = lax.axis_size("tm")
    groups = blocks.bit_length() - 1
    assert blocks == 1 << groups and groups >= 2
    place = lax.axis_index("sens").astype(jnp.int32).reshape(1)
    position = lax.axis_index("tm").astype(jnp.int32)
    bits = jnp.stack([(position >> i) & 1 for i in range(groups)])

    packed = jnp.stack([closed_loop, smoother_gain])
    to_send = half_inputs(place, observations, obs_gain, members, -1, BF16)
    other = lax.ppermute(to_send, "sens", [(0, 1), (1, 0)])
    own = half_inputs(place, observations, obs_gain, members, 1, F32)
    mats = first_powers(packed, transition)
    single, u = second_powers(mats, own, other)
    e_groups, x_groups, d_groups, ends, payload = up(u, mats, single, members)
    maps = all_maps(mats, single, ends, groups)
    block = maps[0]
    mine, got = [ends], []
    for i in range(groups):
        arrived = lax.ppermute(payload, "tm", [(j, j ^ (1 << i)) for j in range(blocks)])
        got.append(arrived)
        names = BLOCK if i == 0 else DOUBLE
        if i < groups - 2:
            ends, payload = join(i, names, bits, ends, arrived, maps[i])
            mine.append(ends)
        elif i == groups - 2:
            ends, payload = last_join(i, names, bits, ends, arrived, maps[i], maps[i + 1])
            mine.append(ends)
    prepared, pre, local = ready(
        bits, initial_mean, u, e_groups, mats, single, maps, mine, got[:-1]
    )
    filtered, smoothed = finish(
        bits, got[-1], prepared, pre, local, x_groups, d_groups, mats, single, block, transition, smoother_gain
    )
    shape = (members, steps, states)
    return filtered.reshape(shape), smoothed.reshape(shape)


def solution(mesh):
    placed = (
        P(("rec", "state"), "tm", "sens"),
        P(None, "sens"),
        P(),
        P(),
        P(),
        P(("rec", "state", "sens"), None),
    )
    return jax.shard_map(
        body,
        mesh=mesh,
        in_specs=placed,
        out_specs=(
            P(("rec", "state", "sens"), "tm", None),
            P(("rec", "state", "sens"), "tm", None),
        ),
        check_vma=False,
    )
```

```python
import jax
import jax.numpy as jnp
from jax import lax
from jax.experimental import pallas as pl
from jax.experimental.pallas import tpu as pltpu
from jax.sharding import PartitionSpec as P

F32 = jnp.float32
BF16 = jnp.bfloat16
LANES = 128
VMEM = pl.BlockSpec(memory_space=pltpu.VMEM)
SMEM = pl.BlockSpec(memory_space=pltpu.SMEM)
ANY = pl.BlockSpec(memory_space=pl.ANY)
PARAMS = pltpu.CompilerParams(vmem_limit_bytes=24 * 2**20)
WIDE = pltpu.CompilerParams(vmem_limit_bytes=54 * 2**20)


def halves(x):
    high = x.astype(BF16)
    return high, (x - high.astype(F32)).astype(BF16)


def dot(x, y):
    return jnp.dot(x, y, preferred_element_type=F32)


def dot_nt(x, y):
    return lax.dot_general(x, y, (((1,), (1,)), ((), ())), preferred_element_type=F32)


def mul(x, y):
    return muls((x, y))


def muls(*terms):
    left, right = [], []
    for x, y in terms:
        left += [x[0], x[1], x[0]]
        right += [y[0], y[0], y[1]]
    return dot(jnp.concatenate(left, 1), jnp.concatenate(right, 0))


class Both:
    def __init__(self, first, second):
        self.stacks = first, second

    def of(self, name):
        return self.stacks[0] if name in self.stacks[0].place else self.stacks[1]

    def put(self, name, value):
        return self.of(name).put(name, value)

    def __getitem__(self, name):
        return self.of(name)[name]


class Stack:
    def __init__(self, names, ref):
        self.place = {name: i for i, name in enumerate(names)}
        self.ref = ref

    def put(self, name, value):
        pair = halves(value)
        self.copy(name, pair)
        return pair

    def copy(self, name, pair):
        self.ref[self.place[name], 0] = pair[0]
        self.ref[self.place[name], 1] = pair[1]

    def __getitem__(self, name):
        return self.ref[self.place[name], 0], self.ref[self.place[name], 1]


def stack_shape(names, n):
    return jax.ShapeDtypeStruct((len(names), 2, n, n), BF16)


def cost(flops):
    return pl.CostEstimate(flops=int(flops), bytes_accessed=0, transcendentals=0)


def split_cols(held, row, product):
    rows = product.shape[0]
    for j in range(held.shape[0]):
        held[j, pl.ds(row, rows)] = product[:, j * LANES : (j + 1) * LANES]


def by_step(held, out, members, steps):
    for t in range(steps):
        for j in range(held.shape[0]):
            step = held.at[j][pl.ds(t, members, stride=steps)]
            out[pl.ds(t * members, members), pl.ds(j * LANES, LANES)] = step.astype(out.dtype)


FIRST = ("a1", "a2", "a3", "a4", "g1", "g2", "g3", "g4", "w", "b")
SECOND = ("a8", "a12", "g8", "g12", "C0", "C1", "C2", "C3", "k4")
BLOCK = ("a", "g", "k", "c", "V0", "V1", "V2")
DOUBLE = ("a", "g", "k", "c")
TOP = ("a", "g", "k", "wg", "c2")
READY = ("Zx", "Zd")


def first_powers(loop, gain, transition):
    n = loop.shape[0]

    def kernel(loop, gain, tr, out, token):
        token[...] = jnp.zeros(token.shape, F32)
        m = Stack(FIRST, out)
        a1 = m.put("a1", loop[...].T)
        g_full = gain[...].T
        g1 = m.put("g1", g_full)
        w = m.put("w", dot(tr[...].T, g1[0]))
        a2, g2 = m.put("a2", mul(a1, a1)), m.put("g2", mul(g1, g1))
        m.put("b", g_full - mul(w, g1))
        m.put("a3", mul(a2, a1))
        m.put("a4", mul(a2, a2))
        m.put("g3", mul(g2, g1))
        m.put("g4", mul(g2, g2))

    return pl.pallas_call(
        kernel,
        out_shape=(stack_shape(FIRST, n), jax.ShapeDtypeStruct((8, LANES), F32)),
        in_specs=[VMEM] * 3,
        out_specs=(VMEM, VMEM),
        compiler_params=PARAMS,
        cost_estimate=cost(1e9),
        name="first_powers",
    )(loop, gain, transition)


def second_powers(first, own, other):
    n = first.shape[2]

    def kernel(first_ref, own, other, out, u, held, sem):
        copy = pltpu.make_async_copy(other, held, sem)
        copy.start()
        f, m = Stack(FIRST, first_ref), Stack(SECOND, out)
        a1, a2, a3, a4, g4, b = (f[name] for name in ("a1", "a2", "a3", "a4", "g4", "b"))
        full, beta = [b[0].astype(F32) + b[1].astype(F32)], [b]
        for i in range(1, 4):
            full.append(mul(b, f["g%d" % i]))
            beta.append(m.put("C3", full[i]) if i == 3 else halves(full[i]))
        a8, g8 = m.put("a8", mul(a4, a4)), m.put("g8", mul(g4, g4))
        c0 = m.put("C0", full[0] + muls((a1, beta[1]), (a2, beta[2]), (a3, beta[3])))
        m.put("C1", full[1] + muls((a1, beta[2]), (a2, beta[3])))
        m.put("C2", full[2] + mul(a1, beta[3]))
        m.put("a12", mul(a8, a4))
        m.put("g12", mul(g8, g4))
        m.put("k4", mul(a1, c0))
        copy.wait()
        u[...] = own[...] + held[...].astype(F32)

    return pl.pallas_call(
        kernel,
        out_shape=(stack_shape(SECOND, n), jax.ShapeDtypeStruct(own.shape, F32)),
        in_specs=[VMEM, VMEM, ANY],
        out_specs=(VMEM, VMEM),
        scratch_shapes=[pltpu.VMEM(other.shape, BF16), pltpu.SemaphoreType.DMA],
        compiler_params=PARAMS,
        cost_estimate=cost(1.5e9),
        name="second_powers",
    )(first, own, other)


def other_inputs(place, obs, gain, members):
    steps, sensors = obs.shape[1:]
    states = gain.shape[0]
    rows = members * steps

    def kernel(place, obs, gain, send, og, read, held, stage, sems):
        copies = [
            pltpu.make_async_copy(gain, og, sems.at[0]),
            pltpu.make_async_copy(obs.at[pl.ds((1 - place[0]) * members, members)], read, sems.at[1]),
        ]
        for copy in copies:
            copy.start()
        for copy in copies:
            copy.wait()
        cut = 16
        for i in range(members // cut):
            part = read[pl.ds(i * cut, cut)].reshape(cut * steps, sensors)
            split_cols(held, i * cut * steps, dot_nt(part, og[...]))
        by_step(held, stage, members, steps)
        last = pltpu.make_async_copy(stage, send, sems.at[2])
        last.start()
        last.wait()

    return pl.pallas_call(
        kernel,
        out_shape=jax.ShapeDtypeStruct((rows, states), BF16),
        in_specs=[SMEM, ANY, ANY],
        out_specs=ANY,
        scratch_shapes=[
            pltpu.VMEM(gain.shape, BF16),
            pltpu.VMEM((members, steps, sensors), BF16),
            pltpu.VMEM((states // LANES, rows, LANES), F32),
            pltpu.VMEM((rows, states), BF16),
            pltpu.SemaphoreType.DMA((3,)),
        ],
        compiler_params=WIDE,
        cost_estimate=cost(5e8),
        name="other_inputs",
    )(place, obs, gain)


def own_inputs(place, obs, gain, after, members):
    steps, sensors = obs.shape[1:]
    states = gain.shape[0]
    cut = 16

    def kernel(place, obs, gain, _, out, held):
        for i in range(members // cut):
            part = obs[pl.ds(place[0] * members + i * cut, cut)].reshape(cut * steps, sensors)
            split_cols(held, i * cut * steps, dot_nt(part, gain[...]))
        by_step(held, out, members, steps)

    return pl.pallas_call(
        kernel,
        out_shape=jax.ShapeDtypeStruct((members * steps, states), F32),
        in_specs=[SMEM, VMEM, VMEM, ANY],
        out_specs=VMEM,
        scratch_shapes=[pltpu.VMEM((states // LANES, members * steps, LANES), F32)],
        compiler_params=PARAMS,
        cost_estimate=cost(5e8),
        name="own_inputs",
    )(place, obs, gain, after)


def put_payload(payload, e, h):
    states = e.shape[1]
    payload[:, pl.ds(0, states)] = e.astype(BF16)
    payload[:, pl.ds(states, states)] = h.astype(BF16)


def up(u, first, second, members):
    rows, states = u.shape
    quads = rows // members // 4

    def kernel(u, first_ref, second_ref, e_out, x_out, d_out, ends, payload):
        f = s = Both(Stack(FIRST, first_ref), Stack(SECOND, second_ref))
        u = u[...].reshape(quads, 4, members, states)
        full = [u[:, j].reshape(-1, states) for j in range(4)]
        pairs = [halves(x) for x in full]
        e = full[3] + muls((pairs[2], f["a1"]), (pairs[1], f["a2"]), (pairs[0], f["a3"]))
        h = muls(*((pairs[j], s["C%d" % j]) for j in range(4)))
        e_out[...] = e
        cut = lambda x, q: x[q * members : (q + 1) * members]
        ah = [f["a4"], s["a8"], s["a12"]]
        gh = [f["g4"], s["g8"], s["g12"]]
        ep = [halves(cut(e, q)) for q in range(quads)]
        entering = [cut(e, 0)]
        for q in range(1, quads):
            entering.append(cut(e, q) + muls(*((ep[p], ah[q - p - 1]) for p in range(q))))
        x = jnp.concatenate(entering[:-1], 0)
        x_out[...] = x
        back_x = mul(halves(x), s["k4"])
        backs = [cut(h, 0)] + [cut(h, q) + cut(back_x, q - 1) for q in range(1, quads)]
        bp = [halves(x) for x in backs]
        handed = [
            backs[q] + muls(*((bp[p], gh[p - q - 1]) for p in range(q + 1, quads))) for q in range(quads - 1)
        ] + [backs[-1]]
        d_out[...] = jnp.concatenate(handed[1:], 0)
        ends[0] = entering[-1]
        ends[1] = handed[0]
        put_payload(payload, entering[-1], handed[0])

    return pl.pallas_call(
        kernel,
        out_shape=(
            jax.ShapeDtypeStruct((quads * members, states), F32),
            jax.ShapeDtypeStruct(((quads - 1) * members, states), F32),
            jax.ShapeDtypeStruct(((quads - 1) * members, states), F32),
            jax.ShapeDtypeStruct((2, members, states), F32),
            jax.ShapeDtypeStruct((members, 2 * states), BF16),
        ),
        in_specs=[VMEM] * 3,
        out_specs=(VMEM,) * 5,
        compiler_params=PARAMS,
        cost_estimate=cost(2e9),
        name="up",
    )(u, first, second)


def fill_block(f, mats):
    k4, a4, g4, a8, g8 = f["k4"], f["a4"], f["g4"], f["a8"], f["g8"]
    full = [mul(x, k4) for x in (a4, a8, f["a12"])]
    t = [halves(x) for x in full]
    mats.put("a", mul(a8, a8))
    g = mats.put("g", mul(g8, g8))
    k = k4[0].astype(F32) + k4[1].astype(F32)
    k = mats.put("k", k + muls((t[0], g4), (t[1], g8), (t[2], f["g12"])))
    mats.put("V0", full[0] + muls((t[1], g4), (t[2], g8)))
    mats.put("V1", full[1] + mul(t[2], g4))
    mats.copy("V2", t[2])
    mats.put("c", mul(k, g))


def fill_double(w, s, mats, top):
    a, g, k, c = s["a"], s["g"], s["k"], s["c"]
    mats.put("a", mul(a, a))
    g = mats.put("g", mul(g, g))
    k2 = mats.put("k", k[0].astype(F32) + k[1].astype(F32) + mul(a, c))
    if top:
        wg = mats.put("wg", mul(w, g))
        mats.put("c2", c[0].astype(F32) + c[1].astype(F32) + mul(a, wg))
    else:
        mats.put("c", mul(k2, g))


def all_maps(first, second, after, groups):
    n = first.shape[2]
    names = [BLOCK] + [DOUBLE] * (groups - 2) + [TOP]

    def kernel(first_ref, second_ref, _, block):
        f = Both(Stack(FIRST, first_ref), Stack(SECOND, second_ref))
        m = Stack(BLOCK, block)
        fill_block(f, m)

    def both_kernel(first_ref, second_ref, _, block, top):
        f = Both(Stack(FIRST, first_ref), Stack(SECOND, second_ref))
        m = Stack(BLOCK, block)
        fill_block(f, m)
        fill_double(f["w"], m, Stack(TOP, top), True)

    joined = groups == 2
    shapes = [stack_shape(names[i], n) for i in range(2 if joined else 1)]
    maps = pl.pallas_call(
        both_kernel if joined else kernel,
        out_shape=shapes,
        in_specs=[VMEM, VMEM, ANY],
        out_specs=[VMEM] * len(shapes),
        compiler_params=PARAMS,
        cost_estimate=cost(1.2e9),
        name="block_maps",
    )(first, second, after)
    maps = list(maps)
    while len(maps) < groups:
        maps.append(double_maps(names[len(maps) - 1], maps[-1], first, len(maps) == groups - 1))
    return maps


def double_maps(names, given, first, top):
    n = given.shape[2]
    kept = TOP if top else DOUBLE

    def kernel(given_ref, first_ref, out):
        fill_double(Stack(FIRST, first_ref)["w"], Stack(names, given_ref), Stack(kept, out), top)

    return pl.pallas_call(
        kernel,
        out_shape=stack_shape(kept, n),
        in_specs=[VMEM] * 2,
        out_specs=VMEM,
        compiler_params=PARAMS,
        cost_estimate=cost(4e8),
        name="double_maps",
    )(given, first)


def sides(bit, mine, got):
    states = mine.shape[2]
    got_e = got[:, pl.ds(0, states)].astype(F32)
    got_h = got[:, pl.ds(states, states)].astype(F32)
    right = bit > 0
    el, er = jnp.where(right, got_e, mine[0]), jnp.where(right, mine[0], got_e)
    hl, hr = jnp.where(right, got_h, mine[1]), jnp.where(right, mine[1], got_h)
    return el, er, hl, hr


def join(level, names, bits, mine, got, mats):
    def kernel(bits, mine, got, mats_ref, ends, payload):
        m = Stack(names, mats_ref)
        el, er, hl, hr = sides(bits[level], mine, got)
        pair = halves(el)
        e = mul(pair, m["a"]) + er
        h = hl + muls((halves(hr), m["g"]), (pair, m["c"]))
        ends[0] = e
        ends[1] = h
        put_payload(payload, e, h)

    return pl.pallas_call(
        kernel,
        out_shape=(jax.ShapeDtypeStruct(mine.shape, F32), jax.ShapeDtypeStruct(got.shape, BF16)),
        in_specs=[SMEM, VMEM, VMEM, VMEM],
        out_specs=(VMEM, VMEM),
        compiler_params=PARAMS,
        cost_estimate=cost(1e8),
        name="join",
    )(bits, mine, got, mats)


def last_join(level, names, bits, mine, got, mats, top_mats):
    members, states = mine.shape[1:]

    def kernel(bits, mine, got, mats_ref, top_ref, end, payload):
        m, t = Stack(names, mats_ref), Stack(TOP, top_ref)
        el, er, hl, hr = sides(bits[level], mine, got)
        pair = halves(el)
        e = er + mul(pair, m["a"])
        handed = hl + muls((halves(hr), m["g"]), (pair, t["c2"]), (halves(er), t["wg"]))
        end[0] = e
        payload[...] = jnp.where(bits[level + 1] > 0, handed, e).astype(BF16)

    return pl.pallas_call(
        kernel,
        out_shape=(
            jax.ShapeDtypeStruct((1, members, states), F32),
            jax.ShapeDtypeStruct((members, states), BF16),
        ),
        in_specs=[SMEM] + [VMEM] * 4,
        out_specs=(VMEM, VMEM),
        compiler_params=PARAMS,
        cost_estimate=cost(1e8),
        name="last_join",
    )(bits, mine, got, mats, top_mats)


def either(flag, x, y):
    return tuple(jnp.where(flag, p, q) for p, q in zip(x, y, strict=True))


def ready(bits, begin, u, e_groups, mats_in, single, maps, ends, got):
    members, states = begin.shape
    rows = u.shape[0]
    quads = rows // members // 4
    top = len(maps) - 1

    def kernel(bits, begin, u, e_groups, mats_ref, single_ref, *refs):
        f = Both(Stack(FIRST, mats_ref), Stack(SECOND, single_ref))
        level_maps = [Stack(BLOCK if i == 0 else TOP if i == top else DOUBLE, refs[i]) for i in range(top + 1)]
        mine = refs[top + 1 : 2 * top + 2]
        arrived = refs[2 * top + 2 : 3 * top + 2]
        out_ref, pre, local = refs[3 * top + 2 :]
        mats = Stack(READY, out_ref)
        unit = halves(jnp.eye(states, dtype=F32))
        none = tuple(jnp.zeros_like(x) for x in unit)
        zero = jnp.zeros((members, states), F32)
        p, q, r, px, pd = unit, unit, none, zero, zero
        for i in range(top):
            m = level_maps[i]
            right = bits[i] > 0
            el, _, _, hr = sides(bits[i], mine[i], arrived[i])
            elp = halves(el)
            hand = mul(elp, m["k"]) + hr
            ak = halves(mul(m["a"], m["k"]))
            if i == 0:
                p, q, r = either(right, m["a"], unit), either(right, unit, m["g"]), either(right, none, ak)
                px, pd = jnp.where(right, el, zero), jnp.where(right, zero, hand)
            else:
                px, pd = (
                    jnp.where(right, mul(elp, p) + px, px),
                    jnp.where(right, mul(elp, r) + pd, mul(halves(hand), q) + pd),
                )
                r = either(
                    right,
                    halves(mul(m["a"], r)),
                    halves(mul(ak, q) + r[0].astype(F32) + r[1].astype(F32)),
                )
                p, q = either(right, halves(mul(m["a"], p)), p), either(right, q, halves(mul(m["g"], q)))
        m = level_maps[top]
        right = bits[top] > 0
        w = f["w"]
        x0 = begin[...]
        own_e = mine[top][0]
        aw = halves(mul(m["a"], w))
        middle = mul(halves(x0), m["a"]) + jnp.where(right, zero, own_e)
        middle_p = halves(middle)
        far = halves(mul(aw, m["g"]) + m["k"][0].astype(F32) + m["k"][1].astype(F32))
        x_in = jnp.where(right, middle, x0)
        d_in = mul(middle_p, either(right, aw, far)) + jnp.where(right, mul(halves(own_e), w), zero)
        x_in_p = halves(x_in)
        pre[0] = mul(x_in_p, p) + px
        pre[1] = muls((halves(d_in), q), (x_in_p, r)) + pd
        mats.copy("Zx", either(right, p, none))
        near = halves(mul(aw, q) + r[0].astype(F32) + r[1].astype(F32))
        mats.copy("Zd", either(right, near, q))
        v = u[...].reshape(quads, 4, members, states)
        part = [v[:, j].reshape(-1, states) for j in range(3)]
        pairs = [halves(x) for x in part[:2]]
        local[0] = part[0]
        local[1] = part[1] + mul(pairs[0], f["a1"])
        local[2] = part[2] + muls((pairs[1], f["a1"]), (pairs[0], f["a2"]))
        local[3] = e_groups[...]

    return pl.pallas_call(
        kernel,
        out_shape=(
            stack_shape(READY, states),
            jax.ShapeDtypeStruct((2, members, states), F32),
            jax.ShapeDtypeStruct((4, quads * members, states), F32),
        ),
        in_specs=[SMEM] + [VMEM] * (5 + len(maps) + len(ends) + len(got)),
        out_specs=(VMEM,) * 3,
        compiler_params=PARAMS,
        cost_estimate=cost(3e9),
        name="ready",
    )(bits, begin, u, e_groups, mats_in, single, *maps, *ends, *got)


def finish(bits, got, prepared, pre, local, x_groups, d_groups, mats, single, block, transition, gain):
    members, states = pre.shape[1:]
    quads = local.shape[1] // members
    steps = 4 * quads
    groups = bits.shape[0]

    def kernel(bits, got, ready_ref, pre, local, xg, dg, mats_ref, single_ref, block_ref, tr, ga, *refs):
        filtered, smoothed, filtered_held, smoothed_held, sems = refs
        z, m = Stack(READY, ready_ref), Stack(BLOCK, block_ref)
        f = s = Both(Stack(FIRST, mats_ref), Stack(SECOND, single_ref))
        arrived = got[...]
        exact = lambda x, y: dot(jnp.concatenate([x, x], 1), jnp.concatenate([y[0], y[1]], 0))
        x = exact(arrived, z["Zx"]) + pre[0]
        d = exact(arrived, z["Zd"]) + pre[1]
        xp, dp = halves(x), halves(d)
        ah, gh = [f["a4"], s["a8"], s["a12"]], [f["g4"], s["g8"], s["g12"]]
        xs, ds = [x], []
        for q in range(1, quads):
            part = pl.ds((q - 1) * members, members)
            xs.append(xg[part] + mul(xp, ah[q - 1]))
            ds.append(dg[part] + muls((dp, gh[quads - q - 1]), (xp, m["V%d" % (q - 1)])))
        x = jnp.concatenate(xs, 0)
        d = jnp.concatenate(ds + [d], 0)
        xp = halves(x)
        low = ga[...].astype(BF16)
        final = bits[0] > 0
        for i in range(1, groups):
            final = jnp.logical_and(final, bits[i] > 0)

        def write(held, j, value):
            for q in range(quads):
                for c in range(held.shape[0]):
                    piece = value[q * members : (q + 1) * members, c * LANES : (c + 1) * LANES]
                    held.at[c][pl.ds(4 * q + j, members, stride=steps)] = piece

        def send(held, out, sem):
            copies = []
            for c in range(held.shape[0]):
                copies.append(pltpu.make_async_copy(held.at[c], out.at[:, pl.ds(c * LANES, LANES)], sem.at[c]))
                copies[-1].start()
            return copies

        states_of = []
        for j in range(4):
            value = local[j] + mul(xp, f["a%d" % (j + 1)])
            states_of.append(value)
            write(filtered_held, j, value)
        copies = send(filtered_held, filtered, sems.at[0])
        adjusted = []
        for j in range(4):
            predicted = dot_nt(states_of[j].astype(BF16), tr[...]).astype(BF16)
            adjusted.append(states_of[j] - dot_nt(predicted, low))
        result = adjusted[3] + d
        tail = (quads - 1) * members
        result = jnp.concatenate([result[:tail], jnp.where(final, states_of[3][tail:], result[tail:])], 0)
        write(smoothed_held, 3, result)
        later = [halves(adjusted[1]), halves(adjusted[2]), halves(result)]
        for j in range(3):
            handed = muls(*((later[i - 1], f["g%d" % (i - j)]) for i in range(j + 1, 4)))
            write(smoothed_held, j, adjusted[j] + handed)
        copies += send(smoothed_held, smoothed, sems.at[1])
        for copy in copies:
            copy.wait()

    return pl.pallas_call(
        kernel,
        out_shape=(jax.ShapeDtypeStruct((members * steps, states), F32),) * 2,
        in_specs=[SMEM] + [VMEM] * 11,
        out_specs=(ANY,) * 2,
        scratch_shapes=[
            pltpu.VMEM((states // LANES, members * steps, LANES), F32),
            pltpu.VMEM((states // LANES, members * steps, LANES), F32),
            pltpu.SemaphoreType.DMA((2, states // LANES)),
        ],
        compiler_params=PARAMS,
        cost_estimate=cost(3e9),
        name="finish",
    )(bits, got, prepared, pre, local, x_groups, d_groups, mats, single, block, transition, gain)


def body(observations, obs_gain, closed_loop, transition, smoother_gain, initial_mean):
    members, states = initial_mean.shape
    steps = observations.shape[1]
    assert steps == 16
    blocks = lax.axis_size("tm")
    groups = blocks.bit_length() - 1
    assert blocks == 1 << groups and groups >= 2
    place = lax.axis_index("sens").astype(jnp.int32).reshape(1)
    position = lax.axis_index("tm").astype(jnp.int32)
    bits = jnp.stack([(position >> i) & 1 for i in range(groups)])

    to_send = other_inputs(place, observations, obs_gain, members)
    other = lax.ppermute(to_send, "sens", [(0, 1), (1, 0)])
    mats, token = first_powers(closed_loop, smoother_gain, transition)
    own = own_inputs(place, observations, obs_gain, token, members)
    single, u = second_powers(mats, own, other)
    e_groups, x_groups, d_groups, ends, payload = up(u, mats, single, members)
    maps = all_maps(mats, single, ends, groups)
    block = maps[0]
    mine, got = [ends], []
    for i in range(groups):
        arrived = lax.ppermute(payload, "tm", [(j, j ^ (1 << i)) for j in range(blocks)])
        got.append(arrived)
        names = BLOCK if i == 0 else DOUBLE
        if i < groups - 2:
            ends, payload = join(i, names, bits, ends, arrived, maps[i])
            mine.append(ends)
        elif i == groups - 2:
            ends, payload = last_join(i, names, bits, ends, arrived, maps[i], maps[i + 1])
            mine.append(ends)
    prepared, pre, local = ready(
        bits, initial_mean, u, e_groups, mats, single, maps, mine, got[:-1]
    )
    filtered, smoothed = finish(
        bits, got[-1], prepared, pre, local, x_groups, d_groups, mats, single, block, transition, smoother_gain
    )
    shape = (members, steps, states)
    return filtered.reshape(shape), smoothed.reshape(shape)


def solution(mesh):
    placed = (
        P(("rec", "state"), "tm", "sens"),
        P(None, "sens"),
        P(),
        P(),
        P(),
        P(("rec", "state", "sens"), None),
    )
    return jax.shard_map(
        body,
        mesh=mesh,
        in_specs=placed,
        out_specs=(
            P(("rec", "state", "sens"), "tm", None),
            P(("rec", "state", "sens"), "tm", None),
        ),
        check_vma=False,
    )
```

```python
import jax
import jax.numpy as jnp
from jax import lax
from jax.experimental import pallas as pl
from jax.experimental.pallas import tpu as pltpu
from jax.sharding import PartitionSpec as P

F32 = jnp.float32
BF16 = jnp.bfloat16
LANES = 128
FEW = 64
VMEM = pl.BlockSpec(memory_space=pltpu.VMEM)
SMEM = pl.BlockSpec(memory_space=pltpu.SMEM)
ANY = pl.BlockSpec(memory_space=pl.ANY)
PARAMS = pltpu.CompilerParams(vmem_limit_bytes=24 * 2**20)
WIDE = pltpu.CompilerParams(vmem_limit_bytes=54 * 2**20)


def halves(x):
    high = x.astype(BF16)
    return high, (x - high.astype(F32)).astype(BF16)


def dot(x, y):
    return jnp.dot(x, y, preferred_element_type=F32)


def dot_nt(x, y):
    return lax.dot_general(x, y, (((1,), (1,)), ((), ())), preferred_element_type=F32)


def mul(x, y):
    return muls((x, y))


def muls(*terms):
    rows = terms[0][0][0].shape[0]
    if rows <= FEW:
        both = jnp.concatenate([jnp.concatenate(x, 0) for x, _ in terms], 1)
        high = jnp.concatenate([x[0] for x, _ in terms], 1)
        result = dot(both, jnp.concatenate([y[0] for _, y in terms], 0))
        return result[:rows] + result[rows:] + dot(high, jnp.concatenate([y[1] for _, y in terms], 0))
    left, right = [], []
    for x, y in terms:
        left += [x[0], x[1], x[0]]
        right += [y[0], y[0], y[1]]
    return dot(jnp.concatenate(left, 1), jnp.concatenate(right, 0))


class Both:
    def __init__(self, first, second):
        self.stacks = first, second

    def of(self, name):
        return self.stacks[0] if name in self.stacks[0].place else self.stacks[1]

    def put(self, name, value):
        return self.of(name).put(name, value)

    def __getitem__(self, name):
        return self.of(name)[name]


class Stack:
    def __init__(self, names, ref):
        self.place = {name: i for i, name in enumerate(names)}
        self.ref = ref

    def put(self, name, value):
        pair = halves(value)
        self.copy(name, pair)
        return pair

    def copy(self, name, pair):
        self.ref[self.place[name], 0] = pair[0]
        self.ref[self.place[name], 1] = pair[1]

    def __getitem__(self, name):
        return self.ref[self.place[name], 0], self.ref[self.place[name], 1]


def stack_shape(names, n):
    return jax.ShapeDtypeStruct((len(names), 2, n, n), BF16)


def cost(flops):
    return pl.CostEstimate(flops=int(flops), bytes_accessed=0, transcendentals=0)


def split_cols(held, row, product):
    rows = product.shape[0]
    for j in range(held.shape[0]):
        held[j, pl.ds(row, rows)] = product[:, j * LANES : (j + 1) * LANES]


def by_step(held, out, members, steps):
    for t in range(steps):
        for j in range(held.shape[0]):
            step = held.at[j][pl.ds(t, members, stride=steps)]
            out[pl.ds(t * members, members), pl.ds(j * LANES, LANES)] = step.astype(out.dtype)


FIRST = ("a1", "a2", "a3", "a4", "g1", "g2", "g3", "g4", "w", "b")
SECOND = ("a8", "a12", "g8", "g12", "C0", "C1", "C2", "C3", "k4")
BLOCK = ("a", "g", "k", "c", "V0", "V1", "V2")
DOUBLE = ("a", "g", "k", "c")
TOP = ("a", "g", "k", "wg", "c2")
READY = ("Zx", "Zd")


def first_powers(loop, gain, transition):
    n = loop.shape[0]

    def kernel(loop, gain, tr, out, token):
        token[...] = jnp.zeros(token.shape, F32)
        m = Stack(FIRST, out)
        a1 = m.put("a1", loop[...].T)
        g_full = gain[...].T
        g1 = m.put("g1", g_full)
        w = m.put("w", dot(tr[...].T, g1[0]))
        a2, g2 = m.put("a2", mul(a1, a1)), m.put("g2", mul(g1, g1))
        m.put("b", g_full - mul(w, g1))
        m.put("a3", mul(a2, a1))
        m.put("a4", mul(a2, a2))
        m.put("g3", mul(g2, g1))
        m.put("g4", mul(g2, g2))

    return pl.pallas_call(
        kernel,
        out_shape=(stack_shape(FIRST, n), jax.ShapeDtypeStruct((8, LANES), F32)),
        in_specs=[VMEM] * 3,
        out_specs=(VMEM, VMEM),
        compiler_params=PARAMS,
        cost_estimate=cost(1e9),
        name="first_powers",
    )(loop, gain, transition)


def second_powers(first, own, other):
    n = first.shape[2]

    def kernel(first_ref, own, other, out, u, held, sem):
        copy = pltpu.make_async_copy(other, held, sem)
        copy.start()
        f, m = Stack(FIRST, first_ref), Stack(SECOND, out)
        a1, a2, a3, a4, g4, b = (f[name] for name in ("a1", "a2", "a3", "a4", "g4", "b"))
        full, beta = [b[0].astype(F32) + b[1].astype(F32)], [b]
        for i in range(1, 4):
            full.append(mul(b, f["g%d" % i]))
            beta.append(m.put("C3", full[i]) if i == 3 else halves(full[i]))
        a8, g8 = m.put("a8", mul(a4, a4)), m.put("g8", mul(g4, g4))
        c0 = m.put("C0", full[0] + muls((a1, beta[1]), (a2, beta[2]), (a3, beta[3])))
        m.put("C1", full[1] + muls((a1, beta[2]), (a2, beta[3])))
        m.put("C2", full[2] + mul(a1, beta[3]))
        m.put("a12", mul(a8, a4))
        m.put("g12", mul(g8, g4))
        m.put("k4", mul(a1, c0))
        copy.wait()
        u[...] = own[...] + held[...].astype(F32)

    return pl.pallas_call(
        kernel,
        out_shape=(stack_shape(SECOND, n), jax.ShapeDtypeStruct(own.shape, F32)),
        in_specs=[VMEM, VMEM, ANY],
        out_specs=(VMEM, VMEM),
        scratch_shapes=[pltpu.VMEM(other.shape, BF16), pltpu.SemaphoreType.DMA],
        compiler_params=PARAMS,
        cost_estimate=cost(1.5e9),
        name="second_powers",
    )(first, own, other)


def other_inputs(place, obs, gain, members):
    steps, sensors = obs.shape[1:]
    states = gain.shape[0]
    rows = members * steps

    def kernel(place, obs, gain, send, og, read, held, stage, sems):
        copies = [
            pltpu.make_async_copy(gain, og, sems.at[0]),
            pltpu.make_async_copy(obs.at[pl.ds((1 - place[0]) * members, members)], read, sems.at[1]),
        ]
        for copy in copies:
            copy.start()
        for copy in copies:
            copy.wait()
        cut = 16
        for i in range(members // cut):
            part = read[pl.ds(i * cut, cut)].reshape(cut * steps, sensors)
            split_cols(held, i * cut * steps, dot_nt(part, og[...]))
        by_step(held, stage, members, steps)
        last = pltpu.make_async_copy(stage, send, sems.at[2])
        last.start()
        last.wait()

    return pl.pallas_call(
        kernel,
        out_shape=jax.ShapeDtypeStruct((rows, states), BF16),
        in_specs=[SMEM, ANY, ANY],
        out_specs=ANY,
        scratch_shapes=[
            pltpu.VMEM(gain.shape, BF16),
            pltpu.VMEM((members, steps, sensors), BF16),
            pltpu.VMEM((states // LANES, rows, LANES), F32),
            pltpu.VMEM((rows, states), BF16),
            pltpu.SemaphoreType.DMA((3,)),
        ],
        compiler_params=WIDE,
        cost_estimate=cost(5e8),
        name="other_inputs",
    )(place, obs, gain)


def own_inputs(place, obs, gain, after, members):
    steps, sensors = obs.shape[1:]
    states = gain.shape[0]
    cut = 16

    def kernel(place, obs, gain, _, out, held):
        for i in range(members // cut):
            part = obs[pl.ds(place[0] * members + i * cut, cut)].reshape(cut * steps, sensors)
            split_cols(held, i * cut * steps, dot_nt(part, gain[...]))
        by_step(held, out, members, steps)

    return pl.pallas_call(
        kernel,
        out_shape=jax.ShapeDtypeStruct((members * steps, states), F32),
        in_specs=[SMEM, VMEM, VMEM, ANY],
        out_specs=VMEM,
        scratch_shapes=[pltpu.VMEM((states // LANES, members * steps, LANES), F32)],
        compiler_params=PARAMS,
        cost_estimate=cost(5e8),
        name="own_inputs",
    )(place, obs, gain, after)


def put_payload(payload, e, h):
    states = e.shape[1]
    payload[:, pl.ds(0, states)] = e.astype(BF16)
    payload[:, pl.ds(states, states)] = h.astype(BF16)


def up(u, first, second, members):
    rows, states = u.shape
    quads = rows // members // 4

    def kernel(u, first_ref, second_ref, e_out, x_out, d_out, ends, payload):
        f = s = Both(Stack(FIRST, first_ref), Stack(SECOND, second_ref))
        u = u[...].reshape(quads, 4, members, states)
        full = [u[:, j].reshape(-1, states) for j in range(4)]
        pairs = [halves(x) for x in full]
        e = full[3] + muls((pairs[2], f["a1"]), (pairs[1], f["a2"]), (pairs[0], f["a3"]))
        h = muls(*((pairs[j], s["C%d" % j]) for j in range(4)))
        e_out[...] = e
        cut = lambda x, q: x[q * members : (q + 1) * members]
        ah = [f["a4"], s["a8"], s["a12"]]
        gh = [f["g4"], s["g8"], s["g12"]]
        ep = [halves(cut(e, q)) for q in range(quads)]
        entering = [cut(e, 0)]
        for q in range(1, quads):
            entering.append(cut(e, q) + muls(*((ep[p], ah[q - p - 1]) for p in range(q))))
        x = jnp.concatenate(entering[:-1], 0)
        x_out[...] = x
        back_x = mul(halves(x), s["k4"])
        backs = [cut(h, 0)] + [cut(h, q) + cut(back_x, q - 1) for q in range(1, quads)]
        bp = [halves(x) for x in backs]
        handed = [
            backs[q] + muls(*((bp[p], gh[p - q - 1]) for p in range(q + 1, quads))) for q in range(quads - 1)
        ] + [backs[-1]]
        d_out[...] = jnp.concatenate(handed[1:], 0)
        ends[0] = entering[-1]
        ends[1] = handed[0]
        put_payload(payload, entering[-1], handed[0])

    return pl.pallas_call(
        kernel,
        out_shape=(
            jax.ShapeDtypeStruct((quads * members, states), F32),
            jax.ShapeDtypeStruct(((quads - 1) * members, states), F32),
            jax.ShapeDtypeStruct(((quads - 1) * members, states), F32),
            jax.ShapeDtypeStruct((2, members, states), F32),
            jax.ShapeDtypeStruct((members, 2 * states), BF16),
        ),
        in_specs=[VMEM] * 3,
        out_specs=(VMEM,) * 5,
        compiler_params=PARAMS,
        cost_estimate=cost(2e9),
        name="up",
    )(u, first, second)


def fill_block(f, mats):
    k4, a4, g4, a8, g8 = f["k4"], f["a4"], f["g4"], f["a8"], f["g8"]
    full = [mul(x, k4) for x in (a4, a8, f["a12"])]
    t = [halves(x) for x in full]
    mats.put("a", mul(a8, a8))
    g = mats.put("g", mul(g8, g8))
    k = k4[0].astype(F32) + k4[1].astype(F32)
    k = mats.put("k", k + muls((t[0], g4), (t[1], g8), (t[2], f["g12"])))
    mats.put("V0", full[0] + muls((t[1], g4), (t[2], g8)))
    mats.put("V1", full[1] + mul(t[2], g4))
    mats.copy("V2", t[2])
    mats.put("c", mul(k, g))


def fill_double(w, s, mats, top):
    a, g, k, c = s["a"], s["g"], s["k"], s["c"]
    mats.put("a", mul(a, a))
    g = mats.put("g", mul(g, g))
    k2 = mats.put("k", k[0].astype(F32) + k[1].astype(F32) + mul(a, c))
    if top:
        wg = mats.put("wg", mul(w, g))
        mats.put("c2", c[0].astype(F32) + c[1].astype(F32) + mul(a, wg))
    else:
        mats.put("c", mul(k2, g))


def all_maps(first, second, after, groups):
    n = first.shape[2]
    names = [BLOCK] + [DOUBLE] * (groups - 2) + [TOP]

    def kernel(first_ref, second_ref, _, block):
        f = Both(Stack(FIRST, first_ref), Stack(SECOND, second_ref))
        m = Stack(BLOCK, block)
        fill_block(f, m)

    def both_kernel(first_ref, second_ref, _, block, top):
        f = Both(Stack(FIRST, first_ref), Stack(SECOND, second_ref))
        m = Stack(BLOCK, block)
        fill_block(f, m)
        fill_double(f["w"], m, Stack(TOP, top), True)

    joined = groups == 2
    shapes = [stack_shape(names[i], n) for i in range(2 if joined else 1)]
    maps = pl.pallas_call(
        both_kernel if joined else kernel,
        out_shape=shapes,
        in_specs=[VMEM, VMEM, ANY],
        out_specs=[VMEM] * len(shapes),
        compiler_params=PARAMS,
        cost_estimate=cost(1.2e9),
        name="block_maps",
    )(first, second, after)
    maps = list(maps)
    while len(maps) < groups:
        maps.append(double_maps(names[len(maps) - 1], maps[-1], first, len(maps) == groups - 1))
    return maps


def double_maps(names, given, first, top):
    n = given.shape[2]
    kept = TOP if top else DOUBLE

    def kernel(given_ref, first_ref, out):
        fill_double(Stack(FIRST, first_ref)["w"], Stack(names, given_ref), Stack(kept, out), top)

    return pl.pallas_call(
        kernel,
        out_shape=stack_shape(kept, n),
        in_specs=[VMEM] * 2,
        out_specs=VMEM,
        compiler_params=PARAMS,
        cost_estimate=cost(4e8),
        name="double_maps",
    )(given, first)


def bit(position, i):
    return (position[0] >> i) & 1


def sides(side, mine, got):
    states = mine.shape[2]
    got_e = got[:, pl.ds(0, states)].astype(F32)
    got_h = got[:, pl.ds(states, states)].astype(F32)
    right = side > 0
    el, er = jnp.where(right, got_e, mine[0]), jnp.where(right, mine[0], got_e)
    hl, hr = jnp.where(right, got_h, mine[1]), jnp.where(right, mine[1], got_h)
    return el, er, hl, hr


def join(level, names, bits, mine, got, mats):
    def kernel(bits, mine, got, mats_ref, ends, payload):
        m = Stack(names, mats_ref)
        el, er, hl, hr = sides(bit(bits, level), mine, got)
        pair = halves(el)
        e = mul(pair, m["a"]) + er
        h = hl + muls((halves(hr), m["g"]), (pair, m["c"]))
        ends[0] = e
        ends[1] = h
        put_payload(payload, e, h)

    return pl.pallas_call(
        kernel,
        out_shape=(jax.ShapeDtypeStruct(mine.shape, F32), jax.ShapeDtypeStruct(got.shape, BF16)),
        in_specs=[SMEM, VMEM, VMEM, VMEM],
        out_specs=(VMEM, VMEM),
        compiler_params=PARAMS,
        cost_estimate=cost(1e8),
        name="join",
    )(bits, mine, got, mats)


def last_join(level, names, bits, mine, got, mats, top_mats):
    members, states = mine.shape[1:]

    def kernel(bits, mine, got, mats_ref, top_ref, end, payload):
        m, t = Stack(names, mats_ref), Stack(TOP, top_ref)
        el, er, hl, hr = sides(bit(bits, level), mine, got)
        pair = halves(el)
        e = er + mul(pair, m["a"])
        handed = hl + muls((halves(hr), m["g"]), (pair, t["c2"]), (halves(er), t["wg"]))
        end[0] = e
        payload[...] = jnp.where(bit(bits, level + 1) > 0, handed, e).astype(BF16)

    return pl.pallas_call(
        kernel,
        out_shape=(
            jax.ShapeDtypeStruct((1, members, states), F32),
            jax.ShapeDtypeStruct((members, states), BF16),
        ),
        in_specs=[SMEM] + [VMEM] * 4,
        out_specs=(VMEM, VMEM),
        compiler_params=PARAMS,
        cost_estimate=cost(1e8),
        name="last_join",
    )(bits, mine, got, mats, top_mats)


def either(flag, x, y):
    return tuple(jnp.where(flag, p, q) for p, q in zip(x, y, strict=True))


def ready(bits, begin, u, e_groups, mats_in, single, maps, ends, got):
    members, states = begin.shape
    rows = u.shape[0]
    quads = rows // members // 4
    top = len(maps) - 1

    def kernel(bits, begin, u, e_groups, mats_ref, single_ref, *refs):
        f = Both(Stack(FIRST, mats_ref), Stack(SECOND, single_ref))
        level_maps = [Stack(BLOCK if i == 0 else TOP if i == top else DOUBLE, refs[i]) for i in range(top + 1)]
        mine = refs[top + 1 : 2 * top + 2]
        arrived = refs[2 * top + 2 : 3 * top + 2]
        out_ref, pre, local = refs[3 * top + 2 :]
        mats = Stack(READY, out_ref)
        unit = halves(jnp.eye(states, dtype=F32))
        none = tuple(jnp.zeros_like(x) for x in unit)
        zero = jnp.zeros((members, states), F32)
        p, q, r, px, pd = unit, unit, none, zero, zero
        for i in range(top):
            m = level_maps[i]
            right = bit(bits, i) > 0
            el, _, _, hr = sides(bit(bits, i), mine[i], arrived[i])
            elp = halves(el)
            hand = mul(elp, m["k"]) + hr
            ak = halves(mul(m["a"], m["k"]))
            if i == 0:
                p, q, r = either(right, m["a"], unit), either(right, unit, m["g"]), either(right, none, ak)
                px, pd = jnp.where(right, el, zero), jnp.where(right, zero, hand)
            else:
                px, pd = (
                    jnp.where(right, mul(elp, p) + px, px),
                    jnp.where(right, mul(elp, r) + pd, mul(halves(hand), q) + pd),
                )
                r = either(
                    right,
                    halves(mul(m["a"], r)),
                    halves(mul(ak, q) + r[0].astype(F32) + r[1].astype(F32)),
                )
                p, q = either(right, halves(mul(m["a"], p)), p), either(right, q, halves(mul(m["g"], q)))
        m = level_maps[top]
        right = bit(bits, top) > 0
        w = f["w"]
        x0 = begin[...]
        own_e = mine[top][0]
        aw = halves(mul(m["a"], w))
        middle = mul(halves(x0), m["a"]) + jnp.where(right, zero, own_e)
        middle_p = halves(middle)
        far = halves(mul(aw, m["g"]) + m["k"][0].astype(F32) + m["k"][1].astype(F32))
        x_in = jnp.where(right, middle, x0)
        d_in = mul(middle_p, either(right, aw, far)) + jnp.where(right, mul(halves(own_e), w), zero)
        x_in_p = halves(x_in)
        pre[0] = mul(x_in_p, p) + px
        pre[1] = muls((halves(d_in), q), (x_in_p, r)) + pd
        mats.copy("Zx", either(right, p, none))
        near = halves(mul(aw, q) + r[0].astype(F32) + r[1].astype(F32))
        mats.copy("Zd", either(right, near, q))
        v = u[...].reshape(quads, 4, members, states)
        part = [v[:, j].reshape(-1, states) for j in range(3)]
        pairs = [halves(x) for x in part[:2]]
        local[0] = part[0]
        local[1] = part[1] + mul(pairs[0], f["a1"])
        local[2] = part[2] + muls((pairs[1], f["a1"]), (pairs[0], f["a2"]))
        local[3] = e_groups[...]

    return pl.pallas_call(
        kernel,
        out_shape=(
            stack_shape(READY, states),
            jax.ShapeDtypeStruct((2, members, states), F32),
            jax.ShapeDtypeStruct((4, quads * members, states), F32),
        ),
        in_specs=[SMEM] + [VMEM] * (5 + len(maps) + len(ends) + len(got)),
        out_specs=(VMEM,) * 3,
        compiler_params=PARAMS,
        cost_estimate=cost(3e9),
        name="ready",
    )(bits, begin, u, e_groups, mats_in, single, *maps, *ends, *got)


def finish(groups, bits, got, prepared, pre, local, x_groups, d_groups, mats, single, block, transition, gain):
    members, states = pre.shape[1:]
    quads = local.shape[1] // members
    steps = 4 * quads

    def kernel(bits, got, ready_ref, pre, local, xg, dg, mats_ref, single_ref, block_ref, tr, ga, *refs):
        filtered, smoothed, filtered_held, smoothed_held, sems = refs
        z, m = Stack(READY, ready_ref), Stack(BLOCK, block_ref)
        f = s = Both(Stack(FIRST, mats_ref), Stack(SECOND, single_ref))
        arrived = got[...]
        exact = lambda x, y: dot(jnp.concatenate([x, x], 1), jnp.concatenate([y[0], y[1]], 0))
        x = exact(arrived, z["Zx"]) + pre[0]
        d = exact(arrived, z["Zd"]) + pre[1]
        xp, dp = halves(x), halves(d)
        ah, gh = [f["a4"], s["a8"], s["a12"]], [f["g4"], s["g8"], s["g12"]]
        xs, ds = [x], []
        for q in range(1, quads):
            part = pl.ds((q - 1) * members, members)
            xs.append(xg[part] + mul(xp, ah[q - 1]))
            ds.append(dg[part] + muls((dp, gh[quads - q - 1]), (xp, m["V%d" % (q - 1)])))
        x = jnp.concatenate(xs, 0)
        d = jnp.concatenate(ds + [d], 0)
        xp = halves(x)
        low = ga[...].astype(BF16)
        final = bit(bits, 0) > 0
        for i in range(1, groups):
            final = jnp.logical_and(final, bit(bits, i) > 0)

        def write(held, j, value):
            for q in range(quads):
                for c in range(held.shape[0]):
                    piece = value[q * members : (q + 1) * members, c * LANES : (c + 1) * LANES]
                    held.at[c][pl.ds(4 * q + j, members, stride=steps)] = piece

        def send(held, out, sem):
            copies = []
            for c in range(held.shape[0]):
                copies.append(pltpu.make_async_copy(held.at[c], out.at[:, pl.ds(c * LANES, LANES)], sem.at[c]))
                copies[-1].start()
            return copies

        states_of = []
        for j in range(4):
            value = local[j] + mul(xp, f["a%d" % (j + 1)])
            states_of.append(value)
            write(filtered_held, j, value)
        copies = send(filtered_held, filtered, sems.at[0])
        adjusted = []
        for j in range(4):
            predicted = dot_nt(states_of[j].astype(BF16), tr[...]).astype(BF16)
            adjusted.append(states_of[j] - dot_nt(predicted, low))
        result = adjusted[3] + d
        tail = (quads - 1) * members
        result = jnp.concatenate([result[:tail], jnp.where(final, states_of[3][tail:], result[tail:])], 0)
        write(smoothed_held, 3, result)
        later = [halves(adjusted[1]), halves(adjusted[2]), halves(result)]
        for j in range(3):
            handed = muls(*((later[i - 1], f["g%d" % (i - j)]) for i in range(j + 1, 4)))
            write(smoothed_held, j, adjusted[j] + handed)
        copies += send(smoothed_held, smoothed, sems.at[1])
        for copy in copies:
            copy.wait()

    return pl.pallas_call(
        kernel,
        out_shape=(jax.ShapeDtypeStruct((members * steps, states), F32),) * 2,
        in_specs=[SMEM] + [VMEM] * 11,
        out_specs=(ANY,) * 2,
        scratch_shapes=[
            pltpu.VMEM((states // LANES, members * steps, LANES), F32),
            pltpu.VMEM((states // LANES, members * steps, LANES), F32),
            pltpu.SemaphoreType.DMA((2, states // LANES)),
        ],
        compiler_params=PARAMS,
        cost_estimate=cost(3e9),
        name="finish",
    )(bits, got, prepared, pre, local, x_groups, d_groups, mats, single, block, transition, gain)


def body(observations, obs_gain, closed_loop, transition, smoother_gain, initial_mean):
    members, states = initial_mean.shape
    steps = observations.shape[1]
    assert steps == 16
    blocks = lax.axis_size("tm")
    groups = blocks.bit_length() - 1
    assert blocks == 1 << groups and groups >= 2
    place = lax.axis_index("sens").astype(jnp.int32).reshape(1)
    bits = lax.axis_index("tm").astype(jnp.int32).reshape(1)

    to_send = other_inputs(place, observations, obs_gain, members)
    other = lax.ppermute(to_send, "sens", [(0, 1), (1, 0)])
    mats, token = first_powers(closed_loop, smoother_gain, transition)
    own = own_inputs(place, observations, obs_gain, token, members)
    single, u = second_powers(mats, own, other)
    e_groups, x_groups, d_groups, ends, payload = up(u, mats, single, members)
    maps = all_maps(mats, single, ends, groups)
    block = maps[0]
    mine, got = [ends], []
    for i in range(groups):
        arrived = lax.ppermute(payload, "tm", [(j, j ^ (1 << i)) for j in range(blocks)])
        got.append(arrived)
        names = BLOCK if i == 0 else DOUBLE
        if i < groups - 2:
            ends, payload = join(i, names, bits, ends, arrived, maps[i])
            mine.append(ends)
        elif i == groups - 2:
            ends, payload = last_join(i, names, bits, ends, arrived, maps[i], maps[i + 1])
            mine.append(ends)
    prepared, pre, local = ready(
        bits, initial_mean, u, e_groups, mats, single, maps, mine, got[:-1]
    )
    filtered, smoothed = finish(
        groups, bits, got[-1], prepared, pre, local, x_groups, d_groups, mats, single, block, transition, smoother_gain
    )
    shape = (members, steps, states)
    return filtered.reshape(shape), smoothed.reshape(shape)


def solution(mesh):
    placed = (
        P(("rec", "state"), "tm", "sens"),
        P(None, "sens"),
        P(),
        P(),
        P(),
        P(("rec", "state", "sens"), None),
    )
    return jax.shard_map(
        body,
        mesh=mesh,
        in_specs=placed,
        out_specs=(
            P(("rec", "state", "sens"), "tm", None),
            P(("rec", "state", "sens"), "tm", None),
        ),
        check_vma=False,
    )
```

```python
import jax
import jax.numpy as jnp
from jax import lax
from jax.experimental import pallas as pl
from jax.experimental.pallas import tpu as pltpu
from jax.sharding import PartitionSpec as P

F32 = jnp.float32
BF16 = jnp.bfloat16
LANES = 128
FEW = 256
VMEM = pl.BlockSpec(memory_space=pltpu.VMEM)
SMEM = pl.BlockSpec(memory_space=pltpu.SMEM)
ANY = pl.BlockSpec(memory_space=pl.ANY)
PARAMS = pltpu.CompilerParams(vmem_limit_bytes=24 * 2**20)
WIDE = pltpu.CompilerParams(vmem_limit_bytes=54 * 2**20)


def halves(x):
    high = x.astype(BF16)
    return high, (x - high.astype(F32)).astype(BF16)


def dot(x, y):
    return jnp.dot(x, y, preferred_element_type=F32)


def dot_nt(x, y):
    return lax.dot_general(x, y, (((1,), (1,)), ((), ())), preferred_element_type=F32)


def mul(x, y):
    return muls((x, y))


def muls(*terms):
    rows = terms[0][0][0].shape[0]
    if rows <= FEW:
        both = jnp.concatenate([jnp.concatenate(x, 0) for x, _ in terms], 1)
        high = jnp.concatenate([x[0] for x, _ in terms], 1)
        result = dot(both, jnp.concatenate([y[0] for _, y in terms], 0))
        return result[:rows] + result[rows:] + dot(high, jnp.concatenate([y[1] for _, y in terms], 0))
    left, right = [], []
    for x, y in terms:
        left += [x[0], x[1], x[0]]
        right += [y[0], y[0], y[1]]
    return dot(jnp.concatenate(left, 1), jnp.concatenate(right, 0))


class Both:
    def __init__(self, first, second):
        self.stacks = first, second

    def of(self, name):
        return self.stacks[0] if name in self.stacks[0].place else self.stacks[1]

    def put(self, name, value):
        return self.of(name).put(name, value)

    def __getitem__(self, name):
        return self.of(name)[name]


class Stack:
    def __init__(self, names, ref):
        self.place = {name: i for i, name in enumerate(names)}
        self.ref = ref

    def put(self, name, value):
        pair = halves(value)
        self.copy(name, pair)
        return pair

    def copy(self, name, pair):
        self.ref[self.place[name], 0] = pair[0]
        self.ref[self.place[name], 1] = pair[1]

    def __getitem__(self, name):
        return self.ref[self.place[name], 0], self.ref[self.place[name], 1]


def stack_shape(names, n):
    return jax.ShapeDtypeStruct((len(names), 2, n, n), BF16)


def cost(flops):
    return pl.CostEstimate(flops=int(flops), bytes_accessed=0, transcendentals=0)


def split_cols(held, row, product):
    rows = product.shape[0]
    for j in range(held.shape[0]):
        held[j, pl.ds(row, rows)] = product[:, j * LANES : (j + 1) * LANES]


def by_step(held, out, members, steps):
    for t in range(steps):
        for j in range(held.shape[0]):
            step = held.at[j][pl.ds(t, members, stride=steps)]
            out[pl.ds(t * members, members), pl.ds(j * LANES, LANES)] = step.astype(out.dtype)


FIRST = ("a1", "a2", "a3", "a4", "g1", "g2", "g3", "g4", "w", "b")
SECOND = ("a8", "a12", "g8", "g12", "C0", "C1", "C2", "C3", "k4")
BLOCK = ("a", "g", "k", "c", "V0", "V1", "V2")
DOUBLE = ("a", "g", "k", "c")
TOP = ("a", "g", "k", "wg", "c2")
READY = ("Zx", "Zd")


def first_powers(loop, gain, transition):
    n = loop.shape[0]

    def kernel(loop, gain, tr, out, token):
        token[...] = jnp.zeros(token.shape, F32)
        m = Stack(FIRST, out)
        a1 = m.put("a1", loop[...].T)
        g_full = gain[...].T
        g1 = m.put("g1", g_full)
        w = m.put("w", dot(tr[...].T, g1[0]))
        a2, g2 = m.put("a2", mul(a1, a1)), m.put("g2", mul(g1, g1))
        m.put("b", g_full - mul(w, g1))
        m.put("a3", mul(a2, a1))
        m.put("a4", mul(a2, a2))
        m.put("g3", mul(g2, g1))
        m.put("g4", mul(g2, g2))

    return pl.pallas_call(
        kernel,
        out_shape=(stack_shape(FIRST, n), jax.ShapeDtypeStruct((8, LANES), F32)),
        in_specs=[VMEM] * 3,
        out_specs=(VMEM, VMEM),
        compiler_params=PARAMS,
        cost_estimate=cost(1e9),
        name="first_powers",
    )(loop, gain, transition)


def second_powers(first, own, other):
    n = first.shape[2]

    def kernel(first_ref, own, other, out, u, held, sem):
        copy = pltpu.make_async_copy(other, held, sem)
        copy.start()
        f, m = Stack(FIRST, first_ref), Stack(SECOND, out)
        a1, a2, a3, a4, g4, b = (f[name] for name in ("a1", "a2", "a3", "a4", "g4", "b"))
        full, beta = [b[0].astype(F32) + b[1].astype(F32)], [b]
        for i in range(1, 4):
            full.append(mul(b, f["g%d" % i]))
            beta.append(m.put("C3", full[i]) if i == 3 else halves(full[i]))
        a8, g8 = m.put("a8", mul(a4, a4)), m.put("g8", mul(g4, g4))
        c0 = m.put("C0", full[0] + muls((a1, beta[1]), (a2, beta[2]), (a3, beta[3])))
        m.put("C1", full[1] + muls((a1, beta[2]), (a2, beta[3])))
        m.put("C2", full[2] + mul(a1, beta[3]))
        m.put("a12", mul(a8, a4))
        m.put("g12", mul(g8, g4))
        m.put("k4", mul(a1, c0))
        copy.wait()
        u[...] = own[...] + held[...].astype(F32)

    return pl.pallas_call(
        kernel,
        out_shape=(stack_shape(SECOND, n), jax.ShapeDtypeStruct(own.shape, F32)),
        in_specs=[VMEM, VMEM, ANY],
        out_specs=(VMEM, VMEM),
        scratch_shapes=[pltpu.VMEM(other.shape, BF16), pltpu.SemaphoreType.DMA],
        compiler_params=PARAMS,
        cost_estimate=cost(1.5e9),
        name="second_powers",
    )(first, own, other)


def other_inputs(place, obs, gain, members):
    steps, sensors = obs.shape[1:]
    states = gain.shape[0]
    rows = members * steps

    def kernel(place, obs, gain, send, og, read, held, stage, sems):
        copies = [
            pltpu.make_async_copy(gain, og, sems.at[0]),
            pltpu.make_async_copy(obs.at[pl.ds((1 - place[0]) * members, members)], read, sems.at[1]),
        ]
        for copy in copies:
            copy.start()
        for copy in copies:
            copy.wait()
        cut = 16
        for i in range(members // cut):
            part = read[pl.ds(i * cut, cut)].reshape(cut * steps, sensors)
            split_cols(held, i * cut * steps, dot_nt(part, og[...]))
        by_step(held, stage, members, steps)
        last = pltpu.make_async_copy(stage, send, sems.at[2])
        last.start()
        last.wait()

    return pl.pallas_call(
        kernel,
        out_shape=jax.ShapeDtypeStruct((rows, states), BF16),
        in_specs=[SMEM, ANY, ANY],
        out_specs=ANY,
        scratch_shapes=[
            pltpu.VMEM(gain.shape, BF16),
            pltpu.VMEM((members, steps, sensors), BF16),
            pltpu.VMEM((states // LANES, rows, LANES), F32),
            pltpu.VMEM((rows, states), BF16),
            pltpu.SemaphoreType.DMA((3,)),
        ],
        compiler_params=WIDE,
        cost_estimate=cost(5e8),
        name="other_inputs",
    )(place, obs, gain)


def own_inputs(place, obs, gain, after, members):
    steps, sensors = obs.shape[1:]
    states = gain.shape[0]
    cut = 16

    def kernel(place, obs, gain, _, out, held):
        for i in range(members // cut):
            part = obs[pl.ds(place[0] * members + i * cut, cut)].reshape(cut * steps, sensors)
            split_cols(held, i * cut * steps, dot_nt(part, gain[...]))
        by_step(held, out, members, steps)

    return pl.pallas_call(
        kernel,
        out_shape=jax.ShapeDtypeStruct((members * steps, states), F32),
        in_specs=[SMEM, VMEM, VMEM, ANY],
        out_specs=VMEM,
        scratch_shapes=[pltpu.VMEM((states // LANES, members * steps, LANES), F32)],
        compiler_params=PARAMS,
        cost_estimate=cost(5e8),
        name="own_inputs",
    )(place, obs, gain, after)


def put_payload(payload, e, h):
    states = e.shape[1]
    payload[:, pl.ds(0, states)] = e.astype(BF16)
    payload[:, pl.ds(states, states)] = h.astype(BF16)


def up(u, first, second, members):
    rows, states = u.shape
    quads = rows // members // 4

    def kernel(u, first_ref, second_ref, e_out, x_out, d_out, ends, payload):
        f = s = Both(Stack(FIRST, first_ref), Stack(SECOND, second_ref))
        u = u[...].reshape(quads, 4, members, states)
        full = [u[:, j].reshape(-1, states) for j in range(4)]
        pairs = [halves(x) for x in full]
        e = full[3] + muls((pairs[2], f["a1"]), (pairs[1], f["a2"]), (pairs[0], f["a3"]))
        h = muls(*((pairs[j], s["C%d" % j]) for j in range(4)))
        e_out[...] = e
        cut = lambda x, q: x[q * members : (q + 1) * members]
        ah = [f["a4"], s["a8"], s["a12"]]
        gh = [f["g4"], s["g8"], s["g12"]]
        ep = [halves(cut(e, q)) for q in range(quads)]
        entering = [cut(e, 0)]
        for q in range(1, quads):
            entering.append(cut(e, q) + muls(*((ep[p], ah[q - p - 1]) for p in range(q))))
        x = jnp.concatenate(entering[:-1], 0)
        x_out[...] = x
        back_x = mul(halves(x), s["k4"])
        backs = [cut(h, 0)] + [cut(h, q) + cut(back_x, q - 1) for q in range(1, quads)]
        bp = [halves(x) for x in backs]
        handed = [
            backs[q] + muls(*((bp[p], gh[p - q - 1]) for p in range(q + 1, quads))) for q in range(quads - 1)
        ] + [backs[-1]]
        d_out[...] = jnp.concatenate(handed[1:], 0)
        ends[0] = entering[-1]
        ends[1] = handed[0]
        put_payload(payload, entering[-1], handed[0])

    return pl.pallas_call(
        kernel,
        out_shape=(
            jax.ShapeDtypeStruct((quads * members, states), F32),
            jax.ShapeDtypeStruct(((quads - 1) * members, states), F32),
            jax.ShapeDtypeStruct(((quads - 1) * members, states), F32),
            jax.ShapeDtypeStruct((2, members, states), F32),
            jax.ShapeDtypeStruct((members, 2 * states), BF16),
        ),
        in_specs=[VMEM] * 3,
        out_specs=(VMEM,) * 5,
        compiler_params=PARAMS,
        cost_estimate=cost(2e9),
        name="up",
    )(u, first, second)


def fill_block(f, mats):
    k4, a4, g4, a8, g8 = f["k4"], f["a4"], f["g4"], f["a8"], f["g8"]
    full = [mul(x, k4) for x in (a4, a8, f["a12"])]
    t = [halves(x) for x in full]
    mats.put("a", mul(a8, a8))
    g = mats.put("g", mul(g8, g8))
    k = k4[0].astype(F32) + k4[1].astype(F32)
    k = mats.put("k", k + muls((t[0], g4), (t[1], g8), (t[2], f["g12"])))
    mats.put("V0", full[0] + muls((t[1], g4), (t[2], g8)))
    mats.put("V1", full[1] + mul(t[2], g4))
    mats.copy("V2", t[2])
    mats.put("c", mul(k, g))


def fill_double(w, s, mats, top):
    a, g, k, c = s["a"], s["g"], s["k"], s["c"]
    mats.put("a", mul(a, a))
    g = mats.put("g", mul(g, g))
    k2 = mats.put("k", k[0].astype(F32) + k[1].astype(F32) + mul(a, c))
    if top:
        wg = mats.put("wg", mul(w, g))
        mats.put("c2", c[0].astype(F32) + c[1].astype(F32) + mul(a, wg))
    else:
        mats.put("c", mul(k2, g))


def all_maps(first, second, after, groups):
    n = first.shape[2]
    names = [BLOCK] + [DOUBLE] * (groups - 2) + [TOP]

    def kernel(first_ref, second_ref, _, block):
        f = Both(Stack(FIRST, first_ref), Stack(SECOND, second_ref))
        m = Stack(BLOCK, block)
        fill_block(f, m)

    def both_kernel(first_ref, second_ref, _, block, top):
        f = Both(Stack(FIRST, first_ref), Stack(SECOND, second_ref))
        m = Stack(BLOCK, block)
        fill_block(f, m)
        fill_double(f["w"], m, Stack(TOP, top), True)

    joined = groups == 2
    shapes = [stack_shape(names[i], n) for i in range(2 if joined else 1)]
    maps = pl.pallas_call(
        both_kernel if joined else kernel,
        out_shape=shapes,
        in_specs=[VMEM, VMEM, ANY],
        out_specs=[VMEM] * len(shapes),
        compiler_params=PARAMS,
        cost_estimate=cost(1.2e9),
        name="block_maps",
    )(first, second, after)
    maps = list(maps)
    while len(maps) < groups:
        maps.append(double_maps(names[len(maps) - 1], maps[-1], first, len(maps) == groups - 1))
    return maps


def double_maps(names, given, first, top):
    n = given.shape[2]
    kept = TOP if top else DOUBLE

    def kernel(given_ref, first_ref, out):
        fill_double(Stack(FIRST, first_ref)["w"], Stack(names, given_ref), Stack(kept, out), top)

    return pl.pallas_call(
        kernel,
        out_shape=stack_shape(kept, n),
        in_specs=[VMEM] * 2,
        out_specs=VMEM,
        compiler_params=PARAMS,
        cost_estimate=cost(4e8),
        name="double_maps",
    )(given, first)


def bit(position, i):
    return (position[0] >> i) & 1


def sides(side, mine, got):
    states = mine.shape[2]
    got_e = got[:, pl.ds(0, states)].astype(F32)
    got_h = got[:, pl.ds(states, states)].astype(F32)
    right = side > 0
    el, er = jnp.where(right, got_e, mine[0]), jnp.where(right, mine[0], got_e)
    hl, hr = jnp.where(right, got_h, mine[1]), jnp.where(right, mine[1], got_h)
    return el, er, hl, hr


def join(level, names, bits, mine, got, mats):
    def kernel(bits, mine, got, mats_ref, ends, payload):
        m = Stack(names, mats_ref)
        el, er, hl, hr = sides(bit(bits, level), mine, got)
        pair = halves(el)
        e = mul(pair, m["a"]) + er
        h = hl + muls((halves(hr), m["g"]), (pair, m["c"]))
        ends[0] = e
        ends[1] = h
        put_payload(payload, e, h)

    return pl.pallas_call(
        kernel,
        out_shape=(jax.ShapeDtypeStruct(mine.shape, F32), jax.ShapeDtypeStruct(got.shape, BF16)),
        in_specs=[SMEM, VMEM, VMEM, VMEM],
        out_specs=(VMEM, VMEM),
        compiler_params=PARAMS,
        cost_estimate=cost(1e8),
        name="join",
    )(bits, mine, got, mats)


def last_join(level, names, bits, mine, got, mats, top_mats):
    members, states = mine.shape[1:]

    def kernel(bits, mine, got, mats_ref, top_ref, end, payload):
        m, t = Stack(names, mats_ref), Stack(TOP, top_ref)
        el, er, hl, hr = sides(bit(bits, level), mine, got)
        pair = halves(el)
        e = er + mul(pair, m["a"])
        handed = hl + muls((halves(hr), m["g"]), (pair, t["c2"]), (halves(er), t["wg"]))
        end[0] = e
        payload[...] = jnp.where(bit(bits, level + 1) > 0, handed, e).astype(BF16)

    return pl.pallas_call(
        kernel,
        out_shape=(
            jax.ShapeDtypeStruct((1, members, states), F32),
            jax.ShapeDtypeStruct((members, states), BF16),
        ),
        in_specs=[SMEM] + [VMEM] * 4,
        out_specs=(VMEM, VMEM),
        compiler_params=PARAMS,
        cost_estimate=cost(1e8),
        name="last_join",
    )(bits, mine, got, mats, top_mats)


def either(flag, x, y):
    return tuple(jnp.where(flag, p, q) for p, q in zip(x, y, strict=True))


def ready(bits, begin, u, e_groups, mats_in, single, maps, ends, got):
    members, states = begin.shape
    rows = u.shape[0]
    quads = rows // members // 4
    top = len(maps) - 1

    def kernel(bits, begin, u, e_groups, mats_ref, single_ref, *refs):
        f = Both(Stack(FIRST, mats_ref), Stack(SECOND, single_ref))
        level_maps = [Stack(BLOCK if i == 0 else TOP if i == top else DOUBLE, refs[i]) for i in range(top + 1)]
        mine = refs[top + 1 : 2 * top + 2]
        arrived = refs[2 * top + 2 : 3 * top + 2]
        out_ref, pre, local = refs[3 * top + 2 :]
        mats = Stack(READY, out_ref)
        unit = halves(jnp.eye(states, dtype=F32))
        none = tuple(jnp.zeros_like(x) for x in unit)
        zero = jnp.zeros((members, states), F32)
        p, q, r, px, pd = unit, unit, none, zero, zero
        for i in range(top):
            m = level_maps[i]
            right = bit(bits, i) > 0
            el, _, _, hr = sides(bit(bits, i), mine[i], arrived[i])
            elp = halves(el)
            hand = mul(elp, m["k"]) + hr
            ak = halves(mul(m["a"], m["k"]))
            if i == 0:
                p, q, r = either(right, m["a"], unit), either(right, unit, m["g"]), either(right, none, ak)
                px, pd = jnp.where(right, el, zero), jnp.where(right, zero, hand)
            else:
                px, pd = (
                    jnp.where(right, mul(elp, p) + px, px),
                    jnp.where(right, mul(elp, r) + pd, mul(halves(hand), q) + pd),
                )
                r = either(
                    right,
                    halves(mul(m["a"], r)),
                    halves(mul(ak, q) + r[0].astype(F32) + r[1].astype(F32)),
                )
                p, q = either(right, halves(mul(m["a"], p)), p), either(right, q, halves(mul(m["g"], q)))
        m = level_maps[top]
        right = bit(bits, top) > 0
        w = f["w"]
        x0 = begin[...]
        own_e = mine[top][0]
        aw = halves(mul(m["a"], w))
        middle = mul(halves(x0), m["a"]) + jnp.where(right, zero, own_e)
        middle_p = halves(middle)
        far = halves(mul(aw, m["g"]) + m["k"][0].astype(F32) + m["k"][1].astype(F32))
        x_in = jnp.where(right, middle, x0)
        d_in = mul(middle_p, either(right, aw, far)) + jnp.where(right, mul(halves(own_e), w), zero)
        x_in_p = halves(x_in)
        pre[0] = mul(x_in_p, p) + px
        pre[1] = muls((halves(d_in), q), (x_in_p, r)) + pd
        mats.copy("Zx", either(right, p, none))
        near = halves(mul(aw, q) + r[0].astype(F32) + r[1].astype(F32))
        mats.copy("Zd", either(right, near, q))
        v = u[...].reshape(quads, 4, members, states)
        part = [v[:, j].reshape(-1, states) for j in range(3)]
        pairs = [halves(x) for x in part[:2]]
        local[0] = part[0]
        local[1] = part[1] + mul(pairs[0], f["a1"])
        local[2] = part[2] + muls((pairs[1], f["a1"]), (pairs[0], f["a2"]))
        local[3] = e_groups[...]

    return pl.pallas_call(
        kernel,
        out_shape=(
            stack_shape(READY, states),
            jax.ShapeDtypeStruct((2, members, states), F32),
            jax.ShapeDtypeStruct((4, quads * members, states), F32),
        ),
        in_specs=[SMEM] + [VMEM] * (5 + len(maps) + len(ends) + len(got)),
        out_specs=(VMEM,) * 3,
        compiler_params=PARAMS,
        cost_estimate=cost(3e9),
        name="ready",
    )(bits, begin, u, e_groups, mats_in, single, *maps, *ends, *got)


def finish(groups, bits, got, prepared, pre, local, x_groups, d_groups, mats, single, block, transition, gain):
    members, states = pre.shape[1:]
    quads = local.shape[1] // members
    steps = 4 * quads

    def kernel(bits, got, ready_ref, pre, local, xg, dg, mats_ref, single_ref, block_ref, tr, ga, *refs):
        filtered, smoothed, filtered_held, smoothed_held, sems = refs
        z, m = Stack(READY, ready_ref), Stack(BLOCK, block_ref)
        f = s = Both(Stack(FIRST, mats_ref), Stack(SECOND, single_ref))
        arrived = got[...]
        exact = lambda x, y: dot(jnp.concatenate([x, x], 1), jnp.concatenate([y[0], y[1]], 0))
        x = exact(arrived, z["Zx"]) + pre[0]
        d = exact(arrived, z["Zd"]) + pre[1]
        xp, dp = halves(x), halves(d)
        ah, gh = [f["a4"], s["a8"], s["a12"]], [f["g4"], s["g8"], s["g12"]]
        xs, ds = [x], []
        for q in range(1, quads):
            part = pl.ds((q - 1) * members, members)
            xs.append(xg[part] + mul(xp, ah[q - 1]))
            ds.append(dg[part] + muls((dp, gh[quads - q - 1]), (xp, m["V%d" % (q - 1)])))
        x = jnp.concatenate(xs, 0)
        d = jnp.concatenate(ds + [d], 0)
        xp = halves(x)
        low = ga[...].astype(BF16)
        final = bit(bits, 0) > 0
        for i in range(1, groups):
            final = jnp.logical_and(final, bit(bits, i) > 0)

        def write(held, j, value):
            for q in range(quads):
                for c in range(held.shape[0]):
                    piece = value[q * members : (q + 1) * members, c * LANES : (c + 1) * LANES]
                    held.at[c][pl.ds(4 * q + j, members, stride=steps)] = piece

        def send(held, out, sem):
            copies = []
            for c in range(held.shape[0]):
                copies.append(pltpu.make_async_copy(held.at[c], out.at[:, pl.ds(c * LANES, LANES)], sem.at[c]))
                copies[-1].start()
            return copies

        states_of = []
        for j in range(4):
            value = local[j] + mul(xp, f["a%d" % (j + 1)])
            states_of.append(value)
            write(filtered_held, j, value)
        copies = send(filtered_held, filtered, sems.at[0])
        adjusted = []
        for j in range(4):
            predicted = dot_nt(states_of[j].astype(BF16), tr[...]).astype(BF16)
            adjusted.append(states_of[j] - dot_nt(predicted, low))
        result = adjusted[3] + d
        tail = (quads - 1) * members
        result = jnp.concatenate([result[:tail], jnp.where(final, states_of[3][tail:], result[tail:])], 0)
        write(smoothed_held, 3, result)
        later = [halves(adjusted[1]), halves(adjusted[2]), halves(result)]
        for j in range(3):
            handed = muls(*((later[i - 1], f["g%d" % (i - j)]) for i in range(j + 1, 4)))
            write(smoothed_held, j, adjusted[j] + handed)
        copies += send(smoothed_held, smoothed, sems.at[1])
        for copy in copies:
            copy.wait()

    return pl.pallas_call(
        kernel,
        out_shape=(jax.ShapeDtypeStruct((members * steps, states), F32),) * 2,
        in_specs=[SMEM] + [VMEM] * 11,
        out_specs=(ANY,) * 2,
        scratch_shapes=[
            pltpu.VMEM((states // LANES, members * steps, LANES), F32),
            pltpu.VMEM((states // LANES, members * steps, LANES), F32),
            pltpu.SemaphoreType.DMA((2, states // LANES)),
        ],
        compiler_params=PARAMS,
        cost_estimate=cost(3e9),
        name="finish",
    )(bits, got, prepared, pre, local, x_groups, d_groups, mats, single, block, transition, gain)


def body(observations, obs_gain, closed_loop, transition, smoother_gain, initial_mean):
    members, states = initial_mean.shape
    steps = observations.shape[1]
    assert steps == 16
    blocks = lax.axis_size("tm")
    groups = blocks.bit_length() - 1
    assert blocks == 1 << groups and groups >= 2
    place = lax.axis_index("sens").astype(jnp.int32).reshape(1)
    bits = lax.axis_index("tm").astype(jnp.int32).reshape(1)

    to_send = other_inputs(place, observations, obs_gain, members)
    other = lax.ppermute(to_send, "sens", [(0, 1), (1, 0)])
    mats, token = first_powers(closed_loop, smoother_gain, transition)
    own = own_inputs(place, observations, obs_gain, token, members)
    single, u = second_powers(mats, own, other)
    e_groups, x_groups, d_groups, ends, payload = up(u, mats, single, members)
    maps = all_maps(mats, single, ends, groups)
    block = maps[0]
    mine, got = [ends], []
    for i in range(groups):
        arrived = lax.ppermute(payload, "tm", [(j, j ^ (1 << i)) for j in range(blocks)])
        got.append(arrived)
        names = BLOCK if i == 0 else DOUBLE
        if i < groups - 2:
            ends, payload = join(i, names, bits, ends, arrived, maps[i])
            mine.append(ends)
        elif i == groups - 2:
            ends, payload = last_join(i, names, bits, ends, arrived, maps[i], maps[i + 1])
            mine.append(ends)
    prepared, pre, local = ready(
        bits, initial_mean, u, e_groups, mats, single, maps, mine, got[:-1]
    )
    filtered, smoothed = finish(
        groups, bits, got[-1], prepared, pre, local, x_groups, d_groups, mats, single, block, transition, smoother_gain
    )
    shape = (members, steps, states)
    return filtered.reshape(shape), smoothed.reshape(shape)


def solution(mesh):
    placed = (
        P(("rec", "state"), "tm", "sens"),
        P(None, "sens"),
        P(),
        P(),
        P(),
        P(("rec", "state", "sens"), None),
    )
    return jax.shard_map(
        body,
        mesh=mesh,
        in_specs=placed,
        out_specs=(
            P(("rec", "state", "sens"), "tm", None),
            P(("rec", "state", "sens"), "tm", None),
        ),
        check_vma=False,
    )
```
